128 devices in a mesh: dp: 8 (over z, core), patch: 16 (over x, y).
Axes of the slice: x: 4, y: 4, z: 4, core: 2. Of those that a mesh axis runs over, the one named last changes fastest.
Arguments:
- patches: bfloat16 [32768, 1024], P(('dp', 'patch')), parts along dimension 0, may hold values from -20 to 20
- cls_in: float32 [8, 1024], P('dp'), parts along dimension 0, may hold values from -64 to 64
- w_attn: bfloat16 [3, 1024, 1024], replicated, may hold values from -1 to 1
- w_out: bfloat16 [1024, 1024], replicated, may hold values from -0.1875 to 0.1875
- w_class: bfloat16 [2, 4, 1024, 1024], replicated, may hold values from -1 to 1
Outputs:
- updated: bfloat16 [32768, 1024], P(('dp', 'patch')), parts along dimension 0
- cls_out: float32 [8, 1024], P('dp'), parts along dimension 0
The draws below stay inside these ranges and needn't reach their ends.
There are 8 independent parts, one for each index of `dp`. The reference program is written for one: setup_inputs(seed, part) draws one part's arguments, and reference() takes and returns one part's arrays. A program takes and returns all parts, laid end to end along the dimension named above; an argument that names none is the same for every part. Nothing has to cross between parts.
All inputs are finite; a program needn't handle non-finite values.
Results may differ from the reference program's by a relative error of at most 0.015.
Values may be sent and summed in bfloat16 or wider, within the bound.
No kernel may reach another device: no remote copies, remote signals or barrier semaphores. Data moves between devices by JAX's collectives and lax.ppermute only.
A program may use at most 128 MiB of HBM per device.

```python
import jax
import jax.numpy as jnp
from jax import lax

HEADS = 16
HEAD_DIM = 64
D = 1024
PATCH_DEV = 256
PATCHES = 4096
CA_LAYERS = 2


def patch_field(key):
    first_key, second_key = jax.random.split(jax.random.fold_in(key, 101), 2)
    blocks = PATCHES // PATCH_DEV
    rising = 0.6 + 1.2 * jnp.arange(blocks, dtype=jnp.float32) / max(blocks - 1, 1)
    offsets = jax.random.truncated_normal(second_key, -4.0, 4.0, (blocks, D), jnp.float32) * rising[:, None]
    noise_part = jax.random.truncated_normal(first_key, -6.0, 6.0, (PATCHES, D), jnp.float32)
    return noise_part + jnp.repeat(offsets, PATCH_DEV, axis=0)


def draw_patches(key, part):
    return patch_field(key).astype(jnp.bfloat16)


def draw_cls_in(key, part):
    noise_key = jax.random.fold_in(key, 202)
    return 2.0 * jax.random.truncated_normal(noise_key, -6.0, 6.0, (1, D), jnp.float32)


def drawn_triple(key, leading_shape):
    query_key, key_key, value_key = jax.random.split(key, 3)
    shape = leading_shape + (D, D)
    scaling = D ** (-0.5)
    query_part = jax.random.truncated_normal(query_key, -4.0, 4.0, shape, jnp.float32) * scaling
    key_part = jax.random.truncated_normal(key_key, -4.0, 4.0, shape, jnp.float32) * scaling
    value_part = jax.random.truncated_normal(value_key, -4.0, 4.0, shape, jnp.float32) * scaling
    return (query_part, key_part, value_part)


def draw_w_attn(key, part):
    query_part, key_part, value_part = drawn_triple(jax.random.fold_in(key, 303), ())
    return jnp.stack([query_part, key_part, value_part], axis=0).astype(jnp.bfloat16)


def draw_w_class(key, part):
    query_part, key_part, value_part = drawn_triple(jax.random.fold_in(key, 404), (CA_LAYERS,))
    out_key = jax.random.fold_in(key, 505)
    out_part = jax.random.truncated_normal(out_key, -4.0, 4.0, (CA_LAYERS, D, D), jnp.float32) * D ** (-0.5)
    return jnp.stack([query_part, key_part, value_part, out_part], axis=1).astype(jnp.bfloat16)


def gaussian(stream_key, shape, width, bound, held_as=jnp.bfloat16):
    return jnp.clip(width * jax.random.normal(stream_key, shape, jnp.float32), -bound, bound).astype(held_as)


def setup_inputs(seed: int = 0, part: int = 0) -> dict:
    keys = jax.random.split(jax.random.key(seed), 6)
    part_keys = jax.random.split(jax.random.fold_in(keys[5], part), 6)
    return {
        "patches": draw_patches(jax.random.fold_in(jax.random.fold_in(keys[5], part), 71), part),
        "cls_in": draw_cls_in(jax.random.fold_in(jax.random.fold_in(keys[5], part), 71), part),
        "w_attn": draw_w_attn(jax.random.fold_in(keys[5], 71), part),
        "w_out": gaussian(keys[3], (D, D), D ** -0.5, 0.1875),
        "w_class": draw_w_class(jax.random.fold_in(keys[5], 71), part),
    }


def attend_block(query_rows, key_all, value_all):
    scores = jnp.einsum('qhd,khd->hqk', query_rows.astype(jnp.float32), key_all.astype(jnp.float32), precision=lax.Precision.HIGHEST)
    row_max = jnp.max(scores, axis=-1, keepdims=True)
    exp_terms = jnp.exp(scores - row_max)
    row_total = jnp.sum(exp_terms, axis=-1, keepdims=True)
    probs = exp_terms.astype(jnp.bfloat16)
    outputs = jnp.einsum('hqk,khd->qhd', probs.astype(jnp.float32), value_all.astype(jnp.float32), precision=lax.Precision.HIGHEST)
    return (outputs / jnp.transpose(row_total, (1, 0, 2))).astype(jnp.bfloat16)


def reference(patches, cls_in, w_attn, w_out, w_class):
    queries = (jnp.dot(patches, w_attn[0], preferred_element_type=jnp.float32) * 0.125).astype(jnp.bfloat16)
    key_rows = jnp.dot(patches, w_attn[1], preferred_element_type=jnp.float32).astype(jnp.bfloat16)
    value_rows = jnp.dot(patches, w_attn[2], preferred_element_type=jnp.float32).astype(jnp.bfloat16)
    query_heads = queries.reshape(PATCHES, HEADS, HEAD_DIM)
    key_heads = key_rows.reshape(PATCHES, HEADS, HEAD_DIM)
    value_heads = value_rows.reshape(PATCHES, HEADS, HEAD_DIM)
    block_rows = min(512, PATCHES)
    block_count = PATCHES // block_rows

    def one_block(block_index):
        row_start = block_index * block_rows
        chosen = lax.dynamic_slice_in_dim(query_heads, row_start, block_rows, 0)
        return attend_block(chosen, key_heads, value_heads)

    attended = lax.map(one_block, jnp.arange(block_count, dtype=jnp.int32)).reshape(PATCHES, D)
    updated = (patches.astype(jnp.float32) + jnp.dot(attended, w_out, preferred_element_type=jnp.float32)).astype(jnp.bfloat16)
    cls_token = cls_in
    for class_index in range(CA_LAYERS):
        cls_bf16 = cls_token.astype(jnp.bfloat16)
        class_keys = jnp.dot(updated, w_class[class_index, 1], preferred_element_type=jnp.float32).astype(jnp.bfloat16)
        class_values = jnp.dot(updated, w_class[class_index, 2], preferred_element_type=jnp.float32).astype(jnp.bfloat16)
        class_query = (jnp.dot(cls_bf16, w_class[class_index, 0], preferred_element_type=jnp.float32) * 0.125).astype(jnp.bfloat16)
        class_query = class_query.astype(jnp.float32).reshape(HEADS, HEAD_DIM)
        self_key = jnp.dot(cls_bf16, w_class[class_index, 1], preferred_element_type=jnp.float32).reshape(HEADS, HEAD_DIM)
        self_value = jnp.dot(cls_bf16, w_class[class_index, 2], preferred_element_type=jnp.float32).reshape(HEADS, HEAD_DIM)
        scores = jnp.einsum('hd,khd->hk', class_query, class_keys.astype(jnp.float32).reshape(PATCHES, HEADS, HEAD_DIM), precision=lax.Precision.HIGHEST)
        self_score = jnp.sum(class_query * self_key, axis=-1)
        row_max = jnp.maximum(jnp.max(scores, axis=1), self_score)
        exp_terms = jnp.exp(scores - row_max[:, None])
        self_term = jnp.exp(self_score - row_max)
        row_total = jnp.sum(exp_terms, axis=1) + self_term
        weighted = jnp.einsum('hk,khd->hd', exp_terms, class_values.astype(jnp.float32).reshape(PATCHES, HEADS, HEAD_DIM), precision=lax.Precision.HIGHEST)
        weighted = weighted + self_term[:, None] * self_value
        class_attn = (weighted / row_total[:, None]).reshape(1, D).astype(jnp.bfloat16)
        cls_token = cls_token + jnp.dot(class_attn, w_class[class_index, 3], preferred_element_type=jnp.float32)
    return (updated, cls_token)
```

```python
import functools

import jax
import jax.numpy as jnp
from jax import lax
from jax.experimental import pallas as pl
from jax.experimental.pallas import tpu as pltpu
from jax.sharding import PartitionSpec as P

HEADS = 16
HEAD_DIM = 64
D = 1024
ROWS = 256
PATCHES = 4096
LOG2E = 1.4426950408889634
BF16 = jnp.bfloat16
F32 = jnp.float32
NN = (((1,), (0,)), ((), ()))
NT = (((1,), (1,)), ((), ()))
TN = (((0,), (0,)), ((), ()))
VMEM_LIMIT = 60 * 2**20


def dot(a, b, dims=NN):
    return lax.dot_general(a, b, dims, preferred_element_type=F32)


def whole(shape):
    return pl.BlockSpec(shape, lambda *_: (0,) * len(shape))


def class_weight(layer, kind):
    return pl.BlockSpec((1, 1, D, D), lambda *_: (layer, kind, 0, 0))


def head_mask():
    row = lax.broadcasted_iota(jnp.int32, (HEADS, D), 0)
    lane = lax.broadcasted_iota(jnp.int32, (HEADS, D), 1)
    return lane // HEAD_DIM == row


def split_rows(value):
    high = value.astype(BF16)
    low = (value - high.astype(F32)).astype(BF16)
    return jnp.concatenate([high, low], axis=0)


def fold_halves(value):
    return value[:HEADS] + value[HEADS:]


def spread(column, mask):
    return jnp.sum(jnp.where(mask, column, 0.0), axis=0, keepdims=True)


def to_tile(row):
    return jnp.concatenate([row[:, 128 * j : 128 * (j + 1)] for j in range(8)], axis=0)


def to_row(tile):
    return jnp.concatenate([tile[j : j + 1, :] for j in range(8)], axis=1)


def project_kernel(x_ref, w_ref, out_ref):
    heads_here = out_ref.shape[0]
    x = x_ref[...]
    for kind in range(3):
        y = dot(x, w_ref[kind])
        if kind == 0:
            y = y * (0.125 * LOG2E)
        yt = y.T.astype(BF16)
        for h in range(heads_here):
            out_ref[h, kind * HEAD_DIM : (kind + 1) * HEAD_DIM, :] = yt[
                h * HEAD_DIM : (h + 1) * HEAD_DIM
            ]


def project(patches, w_attn):
    steps = 4
    cols = D // steps
    return pl.pallas_call(
        project_kernel,
        grid=(steps,),
        out_shape=jax.ShapeDtypeStruct((HEADS, 3 * HEAD_DIM, ROWS), BF16),
        in_specs=[
            whole((ROWS, D)),
            pl.BlockSpec((3, D, cols), lambda i: (0, 0, i)),
        ],
        out_specs=pl.BlockSpec((HEADS // steps, 3 * HEAD_DIM, ROWS), lambda i: (i, 0, 0)),
        compiler_params=pltpu.CompilerParams(vmem_limit_bytes=VMEM_LIMIT),
        cost_estimate=pl.CostEstimate(
            flops=2 * ROWS * D * 3 * D, bytes_accessed=8 * 2**20, transcendentals=0
        ),
        name="project",
    )(patches, w_attn)


def attend_kernel(qkv_ref, out_ref, k_s, v_s, s_s, m_s):
    step = pl.program_id(0)
    chunk = 256

    @pl.when(step == 0)
    def _():
        for j in range(HEADS):
            span = slice(j * ROWS, (j + 1) * ROWS)
            k_s[span, :] = qkv_ref[j, 64:128, :].astype(F32).T.astype(BF16)
            v_s[0:64, span] = qkv_ref[j, 128:192, :]
        v_s[64:80, :] = jnp.ones((16, PATCHES), BF16)
        m_s[...] = jnp.zeros_like(m_s)
        s_s[1] = jnp.zeros((PATCHES, ROWS), F32)

    def half(now, before):
        q_t = qkv_ref[jnp.minimum(step, HEADS - 1), 0:64, :]
        top = m_s[before]
        total = jnp.zeros((80, ROWS), F32)
        tops = []
        for c in range(PATCHES // chunk):
            span = slice(c * chunk, (c + 1) * chunk)
            scores = dot(k_s[span, :], q_t)
            s_s[now, span, :] = scores
            tops.append(jnp.max(scores, axis=0, keepdims=True))
            shifted = s_s[before, span, :] - top
            probs = jnp.exp2(shifted.astype(BF16))
            total = total + dot(v_s[:, span], probs)
        m_s[now] = functools.reduce(jnp.maximum, tops)
        out_ref[jnp.maximum(step - 1, 0)] = (total[0:64] / total[64:65]).astype(BF16)

    @pl.when(step % 2 == 0)
    def _():
        half(0, 1)

    @pl.when(step % 2 == 1)
    def _():
        half(1, 0)


def attend(qkv):
    return pl.pallas_call(
        attend_kernel,
        grid=(HEADS + 1,),
        out_shape=jax.ShapeDtypeStruct((HEADS, HEAD_DIM, ROWS), BF16),
        in_specs=[whole((HEADS, 3 * HEAD_DIM, ROWS))],
        out_specs=whole((HEADS, HEAD_DIM, ROWS)),
        scratch_shapes=[
            pltpu.VMEM((PATCHES, HEAD_DIM), BF16),
            pltpu.VMEM((80, PATCHES), BF16),
            pltpu.VMEM((2, PATCHES, ROWS), F32),
            pltpu.VMEM((2, 1, ROWS), F32),
        ],
        compiler_params=pltpu.CompilerParams(vmem_limit_bytes=VMEM_LIMIT),
        cost_estimate=pl.CostEstimate(
            flops=16 * PATCHES * PATCHES * HEAD_DIM, bytes_accessed=2**21, transcendentals=PATCHES**2
        ),
        name="attend",
    )(qkv)


def self_terms(query, cls_bf16, wk, wv, mask):
    self_key = dot(cls_bf16, wk)
    self_value = dot(cls_bf16, wv)
    product = jnp.where(mask, query * self_key, 0.0)
    score = jnp.sum(product, axis=1, keepdims=True) * LOG2E
    return to_tile(self_value), to_tile(spread(score, mask))


def class_query(cls_bf16, wq):
    return (dot(cls_bf16, wq) * 0.125).astype(BF16).astype(F32)


def ahead_kernel(cls_ref, wq_ref, wk_ref, wv_ref, t_ref, self_ref):
    mask = head_mask()
    cls_bf16 = cls_ref[...].astype(BF16)
    query = class_query(cls_bf16, wq_ref[0, 0])
    spread_query = jnp.where(mask, query, 0.0).astype(BF16)
    turned = dot(spread_query, wk_ref[0, 0], NT) * LOG2E
    t_ref[...] = split_rows(turned)
    value, score = self_terms(query, cls_bf16, wk_ref[0, 0], wv_ref[0, 0], mask)
    self_ref[0:8, :] = value
    self_ref[8:16, :] = score


def ahead(cls_in, w_class):
    return pl.pallas_call(
        ahead_kernel,
        grid=(1,),
        out_shape=(
            jax.ShapeDtypeStruct((2 * HEADS, D), BF16),
            jax.ShapeDtypeStruct((16, 128), F32),
        ),
        in_specs=[whole((1, D)), class_weight(0, 0), class_weight(0, 1), class_weight(0, 2)],
        out_specs=(whole((2 * HEADS, D)), whole((16, 128))),
        compiler_params=pltpu.CompilerParams(vmem_limit_bytes=VMEM_LIMIT),
        cost_estimate=pl.CostEstimate(flops=2**28, bytes_accessed=6 * 2**20, transcendentals=0),
        name="ahead",
    )(cls_in, w_class, w_class, w_class)


def partial_out(scores, values, mask, out_ref):
    top = jnp.max(scores, axis=1, keepdims=True)
    terms = jnp.exp2(scores - top)
    total = jnp.sum(terms, axis=1, keepdims=True)
    weighted = fold_halves(dot(split_rows(terms), values)) / total
    row = jnp.sum(jnp.where(mask, weighted, 0.0), axis=0, keepdims=True)
    tile = jnp.concatenate([to_tile(row), to_tile(spread(top + jnp.log2(total), mask))], axis=0)
    for d in range(HEADS):
        out_ref[d] = tile


def combine(parts_ref, self_ref):
    top = self_ref[8:16, :]
    for d in range(HEADS):
        top = jnp.maximum(top, parts_ref[d, 8:16, :])
    weight = jnp.exp2(self_ref[8:16, :] - top)
    total = weight
    value = weight * self_ref[0:8, :]
    for d in range(HEADS):
        weight = jnp.exp2(parts_ref[d, 8:16, :] - top)
        total = total + weight
        value = value + weight * parts_ref[d, 0:8, :]
    return to_row(value / total).astype(BF16)


def update_kernel(ret_ref, x_ref, wo_ref, t_ref, wv_ref, upd_ref, part_ref):
    mask = head_mask()
    attended = ret_ref[...].reshape(D, ROWS)
    updated = (x_ref[...].astype(F32) + dot(attended, wo_ref[...], TN)).astype(BF16)
    upd_ref[...] = updated
    scores = fold_halves(dot(t_ref[...], updated, NT))
    values = dot(updated, wv_ref[0, 0]).astype(BF16)
    partial_out(scores, values, mask, part_ref)


def update(returned, patches, w_out, turned, w_class):
    return pl.pallas_call(
        update_kernel,
        grid=(1,),
        out_shape=(
            jax.ShapeDtypeStruct((ROWS, D), BF16),
            jax.ShapeDtypeStruct((HEADS, 16, 128), F32),
        ),
        in_specs=[
            whole((HEADS, HEAD_DIM, ROWS)),
            whole((ROWS, D)),
            whole((D, D)),
            whole((2 * HEADS, D)),
            class_weight(0, 2),
        ],
        out_specs=(whole((ROWS, D)), whole((HEADS, 16, 128))),
        compiler_params=pltpu.CompilerParams(vmem_limit_bytes=VMEM_LIMIT),
        cost_estimate=pl.CostEstimate(
            flops=4 * ROWS * D * D, bytes_accessed=6 * 2**20, transcendentals=0
        ),
        name="update",
    )(returned, patches, w_out, turned, w_class)


def class_kv_kernel(upd_ref, wk_ref, wv_ref, k_ref, v_ref):
    updated = upd_ref[...]
    k_ref[...] = dot(updated, wk_ref[0, 0]).astype(BF16)
    v_ref[...] = dot(updated, wv_ref[0, 0]).astype(BF16)


def class_kv(updated, w_class):
    return pl.pallas_call(
        class_kv_kernel,
        grid=(1,),
        out_shape=(jax.ShapeDtypeStruct((ROWS, D), BF16),) * 2,
        in_specs=[whole((ROWS, D)), class_weight(1, 1), class_weight(1, 2)],
        out_specs=(whole((ROWS, D)),) * 2,
        compiler_params=pltpu.CompilerParams(vmem_limit_bytes=VMEM_LIMIT),
        cost_estimate=pl.CostEstimate(
            flops=4 * ROWS * D * D, bytes_accessed=6 * 2**20, transcendentals=0
        ),
        name="class_kv",
    )(updated, w_class, w_class)


def middle_kernel(parts_ref, self_ref, cls_ref, wo_ref, wq_ref, k_ref, v_ref, cls_out_ref, q_ref, part_ref):
    mask = head_mask()
    attn = combine(parts_ref, self_ref)
    cls_token = cls_ref[...] + dot(attn, wo_ref[0, 0])
    cls_out_ref[...] = cls_token
    query = class_query(cls_token.astype(BF16), wq_ref[0, 0])
    q_ref[...] = query
    spread_query = jnp.where(mask, query, 0.0).astype(BF16)
    scores = dot(spread_query, k_ref[...], NT) * LOG2E
    partial_out(scores, v_ref[...], mask, part_ref)


def middle(parts, self_part, cls_in, w_class, keys, values):
    return pl.pallas_call(
        middle_kernel,
        grid=(1,),
        out_shape=(
            jax.ShapeDtypeStruct((1, D), F32),
            jax.ShapeDtypeStruct((1, D), F32),
            jax.ShapeDtypeStruct((HEADS, 16, 128), F32),
        ),
        in_specs=[
            whole((HEADS, 16, 128)),
            whole((16, 128)),
            whole((1, D)),
            class_weight(0, 3),
            class_weight(1, 0),
            whole((ROWS, D)),
            whole((ROWS, D)),
        ],
        out_specs=(whole((1, D)), whole((1, D)), whole((HEADS, 16, 128))),
        compiler_params=pltpu.CompilerParams(vmem_limit_bytes=VMEM_LIMIT),
        cost_estimate=pl.CostEstimate(flops=2**28, bytes_accessed=5 * 2**20, transcendentals=0),
        name="middle",
    )(parts, self_part, cls_in, w_class, w_class, keys, values)


def self_kernel(cls_ref, q_ref, wk_ref, wv_ref, self_ref):
    cls_bf16 = cls_ref[...].astype(BF16)
    value, score = self_terms(q_ref[...], cls_bf16, wk_ref[0, 0], wv_ref[0, 0], head_mask())
    self_ref[0:8, :] = value
    self_ref[8:16, :] = score


def self_part(cls_token, query, w_class):
    return pl.pallas_call(
        self_kernel,
        grid=(1,),
        out_shape=jax.ShapeDtypeStruct((16, 128), F32),
        in_specs=[whole((1, D)), whole((1, D)), class_weight(1, 1), class_weight(1, 2)],
        out_specs=whole((16, 128)),
        compiler_params=pltpu.CompilerParams(vmem_limit_bytes=VMEM_LIMIT),
        cost_estimate=pl.CostEstimate(flops=2**27, bytes_accessed=4 * 2**20, transcendentals=0),
        name="self_part",
    )(cls_token, query, w_class, w_class)


def last_kernel(parts_ref, self_ref, cls_ref, wo_ref, out_ref):
    attn = combine(parts_ref, self_ref)
    out_ref[...] = cls_ref[...] + dot(attn, wo_ref[0, 0])


def last(parts, self_terms_1, cls_token, w_class):
    return pl.pallas_call(
        last_kernel,
        grid=(1,),
        out_shape=jax.ShapeDtypeStruct((1, D), F32),
        in_specs=[whole((HEADS, 16, 128)), whole((16, 128)), whole((1, D)), class_weight(1, 3)],
        out_specs=whole((1, D)),
        compiler_params=pltpu.CompilerParams(vmem_limit_bytes=VMEM_LIMIT),
        cost_estimate=pl.CostEstimate(flops=2**27, bytes_accessed=2 * 2**20, transcendentals=0),
        name="last",
    )(parts, self_terms_1, cls_token, w_class)


def exchange(blocks):
    return lax.all_to_all(blocks, "patch", 0, 0)


def per_device(patches, cls_in, w_attn, w_out, w_class):
    qkv = exchange(project(patches, w_attn))
    turned, self_0 = ahead(cls_in, w_class)
    returned = exchange(attend(qkv))
    updated, part_0 = update(returned, patches, w_out, turned, w_class)
    parts_0 = exchange(part_0)
    keys, values = class_kv(updated, w_class)
    cls_1, query_1, part_1 = middle(parts_0, self_0, cls_in, w_class, keys, values)
    parts_1 = exchange(part_1)
    self_1 = self_part(cls_1, query_1, w_class)
    return (updated, last(parts_1, self_1, cls_1, w_class))


def solution(mesh):
    placed = (P(("dp", "patch"), None), P("dp", None), P(), P(), P())
    return jax.shard_map(
        per_device,
        mesh=mesh,
        in_specs=placed,
        out_specs=(P(("dp", "patch"), None), P("dp", None)),
        check_vma=False,
    )
```

```python
import functools

import jax
import jax.numpy as jnp
from jax import lax
from jax.experimental import pallas as pl
from jax.experimental.pallas import tpu as pltpu
from jax.sharding import PartitionSpec as P

HEADS = 16
HEAD_DIM = 64
D = 1024
ROWS = 256
PATCHES = 4096
LOG2E = 1.4426950408889634
BF16 = jnp.bfloat16
F32 = jnp.float32
NN = (((1,), (0,)), ((), ()))
NT = (((1,), (1,)), ((), ()))
TN = (((0,), (0,)), ((), ()))
VMEM_LIMIT = 20 * 2**20
SMALL_LIMIT = 16 * 2**20
LARGE_LIMIT = 52 * 2**20


def dot(a, b, dims=NN):
    return lax.dot_general(a, b, dims, preferred_element_type=F32)


RESIDENT = pl.BlockSpec(memory_space=pltpu.VMEM)
ANYWHERE = pl.BlockSpec(memory_space=pl.ANY)


def call(kernel, name, flops, out_shape, resident, remote=(), scratch=(), hbm_out=0):
    single = not isinstance(out_shape, tuple)
    count = 1 if single else len(out_shape)
    out_specs = (ANYWHERE,) * hbm_out + (RESIDENT,) * (count - hbm_out)
    return pl.pallas_call(
        kernel,
        out_shape=out_shape,
        in_specs=[RESIDENT] * len(resident) + [ANYWHERE] * len(remote),
        out_specs=out_specs[0] if single else out_specs,
        scratch_shapes=scratch,
        compiler_params=pltpu.CompilerParams(
            vmem_limit_bytes=LARGE_LIMIT if remote else SMALL_LIMIT
        ),
        cost_estimate=pl.CostEstimate(flops=flops, bytes_accessed=2**20, transcendentals=0),
        name=name,
    )(*resident, *remote)


SQUARE = pltpu.VMEM((D, D), BF16)


def head_mask():
    row = lax.broadcasted_iota(jnp.int32, (HEADS, D), 0)
    lane = lax.broadcasted_iota(jnp.int32, (HEADS, D), 1)
    return lane // HEAD_DIM == row


def split_rows(value):
    high = value.astype(BF16)
    low = (value - high.astype(F32)).astype(BF16)
    return jnp.concatenate([high, low], axis=0)


def fold_halves(value):
    return value[:HEADS] + value[HEADS:]


def spread(column, mask):
    return jnp.sum(jnp.where(mask, column, 0.0), axis=0, keepdims=True)


def to_tile(row):
    return jnp.concatenate([row[:, 128 * j : 128 * (j + 1)] for j in range(8)], axis=0)


def to_row(tile):
    return jnp.concatenate([tile[j : j + 1, :] for j in range(8)], axis=1)


def project_kernel(x_hbm, w_hbm, out_ref, x_s, w_s, x_sem, w_sem):
    x_copy = pltpu.make_async_copy(x_hbm, x_s, x_sem)
    copies = [pltpu.make_async_copy(w_hbm.at[k], w_s.at[k], w_sem.at[k]) for k in range(3)]
    x_copy.start()
    for copy in copies:
        copy.start()
    x_copy.wait()
    x = x_s[...]
    for kind in range(3):
        copies[kind].wait()
        y = dot(x, w_s[kind])
        if kind == 0:
            y = y * (0.125 * LOG2E)
        yt = y.astype(BF16).T
        for h in range(HEADS):
            out_ref[h, kind * HEAD_DIM : (kind + 1) * HEAD_DIM, :] = yt[
                h * HEAD_DIM : (h + 1) * HEAD_DIM
            ]


def project(patches, w_attn):
    return pl.pallas_call(
        project_kernel,
        out_shape=jax.ShapeDtypeStruct((HEADS, 3 * HEAD_DIM, ROWS), BF16),
        in_specs=[ANYWHERE] * 2,
        out_specs=RESIDENT,
        scratch_shapes=[
            pltpu.VMEM((ROWS, D), BF16),
            pltpu.VMEM((3, D, D), BF16),
            pltpu.SemaphoreType.DMA(()),
            pltpu.SemaphoreType.DMA((3,)),
        ],
        compiler_params=pltpu.CompilerParams(vmem_limit_bytes=62 * 2**20),
        cost_estimate=pl.CostEstimate(
            flops=2 * ROWS * D * 3 * D, bytes_accessed=8 * 2**20, transcendentals=0
        ),
        name="project",
    )(patches, w_attn)


CHUNK = 256
SPANS = [slice(c * CHUNK, (c + 1) * CHUNK) for c in range(PATCHES // CHUNK)]


def attend_kernel(qkv_ref, out_ref, k_s, v_s, s_s):
    for j, span in enumerate(SPANS):
        k_s[span, :] = qkv_ref[j, 64:128, :].T
        v_s[0:64, span] = qkv_ref[j, 128:192, :]
    v_s[64:80, :] = jnp.ones((16, PATCHES), BF16)

    def scores_of(q_t, span, now):
        scores = dot(k_s[span, :], q_t)
        s_s[now, span, :] = scores
        return jnp.max(scores, axis=0, keepdims=True)

    def weigh(span, before, top):
        probs = jnp.exp2((s_s[before, span, :] - top).astype(BF16))
        return dot(v_s[:, span], probs)

    def finish(block, total):
        out_ref[block] = (total[0:64] / total[64:65]).astype(BF16)

    def both(block, now, top):
        q_t = qkv_ref[block, 0:64, :]
        total = jnp.zeros((80, ROWS), F32)
        tops = []
        for span in SPANS:
            tops.append(scores_of(q_t, span, now))
            total = total + weigh(span, 1 - now, top)
        finish(block - 1, total)
        return functools.reduce(jnp.maximum, tops)

    def pair(t, top):
        top = both(2 * t + 1, 1, top)
        return both(2 * t + 2, 0, top)

    q_t = qkv_ref[0, 0:64, :]
    top = functools.reduce(jnp.maximum, [scores_of(q_t, span, 0) for span in SPANS])
    top = lax.fori_loop(0, 7, pair, top)
    top = both(15, 1, top)
    total = jnp.zeros((80, ROWS), F32)
    for span in SPANS:
        total = total + weigh(span, 1, top)
    finish(15, total)


def attend(qkv):
    return pl.pallas_call(
        attend_kernel,
        out_shape=jax.ShapeDtypeStruct((HEADS, HEAD_DIM, ROWS), BF16),
        in_specs=[RESIDENT],
        out_specs=RESIDENT,
        scratch_shapes=[
            pltpu.VMEM((PATCHES, HEAD_DIM), BF16),
            pltpu.VMEM((80, PATCHES), BF16),
            pltpu.VMEM((2, PATCHES, ROWS), F32),
        ],
        compiler_params=pltpu.CompilerParams(vmem_limit_bytes=VMEM_LIMIT),
        cost_estimate=pl.CostEstimate(
            flops=16 * PATCHES * PATCHES * HEAD_DIM, bytes_accessed=2**21, transcendentals=PATCHES**2
        ),
        name="attend",
    )(qkv)


def self_terms(query, cls_bf16, wk, wv, mask):
    self_key = dot(cls_bf16, wk)
    self_value = dot(cls_bf16, wv)
    product = jnp.where(mask, query * self_key, 0.0)
    score = jnp.sum(product, axis=1, keepdims=True) * LOG2E
    return to_tile(self_value), to_tile(spread(score, mask))


def class_query(cls_bf16, wq):
    return (dot(cls_bf16, wq) * 0.125).astype(BF16).astype(F32)


def start_copies(copies):
    copies = [pltpu.make_async_copy(*copy) for copy in copies]
    for copy in copies:
        copy.start()
    return copies


PIECES = 4
PIECE = D // PIECES


def stream(w_hbm, w_s, sems):
    cut = [slice(PIECE * p, PIECE * (p + 1)) for p in range(PIECES)]
    return start_copies([(w_hbm.at[c], w_s.at[c], sems.at[p]) for p, c in enumerate(cut)])


def dot_streamed(a, w_s, copies, turned=False):
    total = None
    for p, copy in enumerate(copies):
        cut = slice(PIECE * p, PIECE * (p + 1))
        copy.wait()
        part = dot(a[cut, :], w_s[cut, :], TN) if turned else dot(a[:, cut], w_s[cut, :])
        total = part if total is None else total + part
    return total


def ahead_kernel(cls_ref, w_hbm, t_ref, self_ref, wq_s, wk_s, wv_s, sems):
    copies = start_copies([(w_hbm.at[0, k], ref, sems.at[k]) for k, ref in enumerate((wq_s, wk_s, wv_s))])
    mask = head_mask()
    cls_bf16 = cls_ref[...].astype(BF16)
    copies[0].wait()
    query = class_query(cls_bf16, wq_s[...])
    spread_query = jnp.where(mask, query, 0.0).astype(BF16)
    copies[1].wait()
    turned = dot(spread_query, wk_s[...], NT) * LOG2E
    t_ref[...] = split_rows(turned)
    copies[2].wait()
    value, score = self_terms(query, cls_bf16, wk_s[...], wv_s[...], mask)
    self_ref[0:8, :] = value
    self_ref[8:16, :] = score


def ahead(cls_in, w_class):
    shapes = (jax.ShapeDtypeStruct((2 * HEADS, D), BF16), jax.ShapeDtypeStruct((16, 128), F32))
    scratch = (SQUARE, SQUARE, SQUARE, pltpu.SemaphoreType.DMA((3,)))
    return call(ahead_kernel, "ahead", 2**30, shapes, (cls_in,), (w_class,), scratch)


def partial_out(scores, values, mask, out_ref):
    top = jnp.max(scores, axis=1, keepdims=True)
    terms = jnp.exp2(scores - top)
    total = jnp.sum(terms, axis=1, keepdims=True)
    weighted = fold_halves(dot(split_rows(terms), values)) / total
    row = jnp.sum(jnp.where(mask, weighted, 0.0), axis=0, keepdims=True)
    tile = jnp.concatenate([to_tile(row), to_tile(spread(top + jnp.log2(total), mask))], axis=0)
    for d in range(HEADS):
        out_ref[d] = tile


def combine(parts_ref, self_ref):
    top = self_ref[8:16, :]
    for d in range(HEADS):
        top = jnp.maximum(top, parts_ref[d, 8:16, :])
    weight = jnp.exp2(self_ref[8:16, :] - top)
    total = weight
    value = weight * self_ref[0:8, :]
    for d in range(HEADS):
        weight = jnp.exp2(parts_ref[d, 8:16, :] - top)
        total = total + weight
        value = value + weight * parts_ref[d, 0:8, :]
    return to_row(value / total).astype(BF16)


def update_kernel(ret_ref, x_ref, t_ref, wo_hbm, w_hbm, upd_hbm, upd_ref, part_ref, wo_s, wv_s, sems, sem):
    wo_copies = stream(wo_hbm, wo_s, sems.at[0])
    wv_copies = stream(w_hbm.at[0, 2], wv_s, sems.at[1])
    mask = head_mask()
    attended = ret_ref[...].reshape(D, ROWS)
    added = dot_streamed(attended, wo_s, wo_copies, turned=True)
    updated = (x_ref[...].astype(F32) + added).astype(BF16)
    upd_ref[...] = updated
    (out_copy,) = start_copies([(upd_ref, upd_hbm, sem)])
    scores = fold_halves(dot(t_ref[...], updated, NT))
    for copy in wv_copies:
        copy.wait()
    values = dot(updated, wv_s[...]).astype(BF16)
    partial_out(scores, values, mask, part_ref)
    out_copy.wait()


def update(returned, patches, w_out, turned, w_class):
    shapes = (
        jax.ShapeDtypeStruct((ROWS, D), BF16),
        jax.ShapeDtypeStruct((ROWS, D), BF16),
        jax.ShapeDtypeStruct((HEADS, 16, 128), F32),
    )
    scratch = (SQUARE, SQUARE, pltpu.SemaphoreType.DMA((2, PIECES)), pltpu.SemaphoreType.DMA(()))
    args = (returned, patches, turned)
    return call(update_kernel, "update", 4 * ROWS * D * D, shapes, args, (w_out, w_class), scratch, 1)


def class_kv_kernel(upd_ref, w_hbm, k_ref, v_ref, wk_s, wv_s, sems):
    copies = start_copies([(w_hbm.at[1, 1], wk_s, sems.at[0]), (w_hbm.at[1, 2], wv_s, sems.at[1])])
    updated = upd_ref[...]
    copies[0].wait()
    k_ref[...] = dot(updated, wk_s[...]).astype(BF16)
    copies[1].wait()
    v_ref[...] = dot(updated, wv_s[...]).astype(BF16)


def class_kv(updated, w_class):
    shapes = (jax.ShapeDtypeStruct((ROWS, D), BF16),) * 2
    scratch = (SQUARE, SQUARE, pltpu.SemaphoreType.DMA((2,)))
    return call(class_kv_kernel, "class_kv", 2**31, shapes, (updated,), (w_class,), scratch)


def middle_kernel(
    parts_ref, self_ref, cls_ref, k_ref, v_ref, w_hbm, cls_out_ref, q_ref, part_ref, wo_s, wq_s, sems
):
    wo_copies = stream(w_hbm.at[0, 3], wo_s, sems.at[0])
    wq_copies = stream(w_hbm.at[1, 0], wq_s, sems.at[1])
    mask = head_mask()
    attn = combine(parts_ref, self_ref)
    cls_token = cls_ref[...] + dot_streamed(attn, wo_s, wo_copies)
    cls_out_ref[...] = cls_token
    query = (dot_streamed(cls_token.astype(BF16), wq_s, wq_copies) * 0.125).astype(BF16).astype(F32)
    q_ref[...] = query
    spread_query = jnp.where(mask, query, 0.0).astype(BF16)
    scores = dot(spread_query, k_ref[...], NT) * LOG2E
    partial_out(scores, v_ref[...], mask, part_ref)


def middle(parts, self_part, cls_in, keys, values, w_class):
    shapes = (
        jax.ShapeDtypeStruct((1, D), F32),
        jax.ShapeDtypeStruct((1, D), F32),
        jax.ShapeDtypeStruct((HEADS, 16, 128), F32),
    )
    args = (parts, self_part, cls_in, keys, values)
    scratch = (SQUARE, SQUARE, pltpu.SemaphoreType.DMA((2, PIECES)))
    return call(middle_kernel, "middle", 2**28, shapes, args, (w_class,), scratch)


def self_kernel(cls_ref, q_ref, w_hbm, self_ref, wk_s, wv_s, sems):
    copies = start_copies([(w_hbm.at[1, 1], wk_s, sems.at[0]), (w_hbm.at[1, 2], wv_s, sems.at[1])])
    cls_bf16 = cls_ref[...].astype(BF16)
    for copy in copies:
        copy.wait()
    value, score = self_terms(q_ref[...], cls_bf16, wk_s[...], wv_s[...], head_mask())
    self_ref[0:8, :] = value
    self_ref[8:16, :] = score


def self_part(cls_token, query, w_class):
    shape = jax.ShapeDtypeStruct((16, 128), F32)
    scratch = (SQUARE, SQUARE, pltpu.SemaphoreType.DMA((2,)))
    return call(self_kernel, "self_part", 2**30, shape, (cls_token, query), (w_class,), scratch)


def last_kernel(parts_ref, self_ref, cls_ref, w_hbm, out_ref, wo_s, sems):
    wo_copies = stream(w_hbm.at[1, 3], wo_s, sems)
    attn = combine(parts_ref, self_ref)
    out_ref[...] = cls_ref[...] + dot_streamed(attn, wo_s, wo_copies)


def last(parts, self_terms_1, cls_token, w_class):
    shape = jax.ShapeDtypeStruct((1, D), F32)
    scratch = (SQUARE, pltpu.SemaphoreType.DMA((PIECES,)))
    args = (parts, self_terms_1, cls_token)
    return call(last_kernel, "last", 2**27, shape, args, (w_class,), scratch)


def exchange(blocks):
    return lax.all_to_all(blocks, "patch", 0, 0)


def per_device(patches, cls_in, w_attn, w_out, w_class):
    qkv = exchange(project(patches, w_attn))
    turned, self_0 = ahead(cls_in, w_class)
    returned = exchange(attend(qkv))
    updated, updated_here, part_0 = update(returned, patches, w_out, turned, w_class)
    parts_0 = exchange(part_0)
    keys, values = class_kv(updated_here, w_class)
    cls_1, query_1, part_1 = middle(parts_0, self_0, cls_in, keys, values, w_class)
    parts_1 = exchange(part_1)
    self_1 = self_part(cls_1, query_1, w_class)
    return (updated, last(parts_1, self_1, cls_1, w_class))


def solution(mesh):
    placed = (P(("dp", "patch"), None), P("dp", None), P(), P(), P())
    return jax.shard_map(
        per_device,
        mesh=mesh,
        in_specs=placed,
        out_specs=(P(("dp", "patch"), None), P("dp", None)),
        check_vma=False,
    )
```

```python
import functools

import jax
import jax.numpy as jnp
from jax import lax
from jax.experimental import pallas as pl
from jax.experimental.pallas import tpu as pltpu
from jax.sharding import PartitionSpec as P

HEADS = 16
HEAD_DIM = 64
D = 1024
ROWS = 256
PATCHES = 4096
LOG2E = 1.4426950408889634
BF16 = jnp.bfloat16
F32 = jnp.float32
NN = (((1,), (0,)), ((), ()))
NT = (((1,), (1,)), ((), ()))
TN = (((0,), (0,)), ((), ()))
VMEM_LIMIT = 14 * 2**20
SMALL_LIMIT = 8 * 2**20
LARGE_LIMIT = 46 * 2**20


def dot(a, b, dims=NN):
    return lax.dot_general(a, b, dims, preferred_element_type=F32)


RESIDENT = pl.BlockSpec(memory_space=pltpu.VMEM)
ANYWHERE = pl.BlockSpec(memory_space=pl.ANY)


def call(kernel, name, flops, out_shape, resident, remote=(), scratch=(), hbm_out=0):
    single = not isinstance(out_shape, tuple)
    count = 1 if single else len(out_shape)
    out_specs = (ANYWHERE,) * hbm_out + (RESIDENT,) * (count - hbm_out)
    return pl.pallas_call(
        kernel,
        out_shape=out_shape,
        in_specs=[RESIDENT] * len(resident) + [ANYWHERE] * len(remote),
        out_specs=out_specs[0] if single else out_specs,
        scratch_shapes=scratch,
        compiler_params=pltpu.CompilerParams(
            vmem_limit_bytes=LARGE_LIMIT if remote else SMALL_LIMIT
        ),
        cost_estimate=pl.CostEstimate(flops=flops, bytes_accessed=2**20, transcendentals=0),
        name=name,
    )(*resident, *remote)


SQUARE = pltpu.VMEM((D, D), BF16)


def head_mask():
    row = lax.broadcasted_iota(jnp.int32, (HEADS, D), 0)
    lane = lax.broadcasted_iota(jnp.int32, (HEADS, D), 1)
    return lane // HEAD_DIM == row


def split_rows(value):
    high = value.astype(BF16)
    low = (value - high.astype(F32)).astype(BF16)
    return jnp.concatenate([high, low], axis=0)


def fold_halves(value):
    return value[:HEADS] + value[HEADS:]


def spread(column, mask):
    return jnp.sum(jnp.where(mask, column, 0.0), axis=0, keepdims=True)


def to_tile(row):
    return jnp.concatenate([row[:, 128 * j : 128 * (j + 1)] for j in range(8)], axis=0)


def to_row(tile):
    return jnp.concatenate([tile[j : j + 1, :] for j in range(8)], axis=1)


def project_kernel(x_hbm, w_hbm, out_ref, x_s, w_s, x_sem, w_sem):
    x_copy = pltpu.make_async_copy(x_hbm, x_s, x_sem)
    copies = [pltpu.make_async_copy(w_hbm.at[k], w_s.at[k], w_sem.at[k]) for k in range(3)]
    x_copy.start()
    for copy in copies:
        copy.start()
    x_copy.wait()
    x = x_s[...]
    for kind in range(3):
        copies[kind].wait()
        y = dot(x, w_s[kind])
        if kind == 0:
            y = y * (0.125 * LOG2E)
        yt = y.astype(BF16).T
        for h in range(HEADS):
            out_ref[h, kind * HEAD_DIM : (kind + 1) * HEAD_DIM, :] = yt[
                h * HEAD_DIM : (h + 1) * HEAD_DIM
            ]


def project(patches, w_attn):
    return pl.pallas_call(
        project_kernel,
        out_shape=jax.ShapeDtypeStruct((HEADS, 3 * HEAD_DIM, ROWS), BF16),
        in_specs=[ANYWHERE] * 2,
        out_specs=RESIDENT,
        scratch_shapes=[
            pltpu.VMEM((ROWS, D), BF16),
            pltpu.VMEM((3, D, D), BF16),
            pltpu.SemaphoreType.DMA(()),
            pltpu.SemaphoreType.DMA((3,)),
        ],
        compiler_params=pltpu.CompilerParams(vmem_limit_bytes=62 * 2**20),
        cost_estimate=pl.CostEstimate(
            flops=2 * ROWS * D * 3 * D, bytes_accessed=8 * 2**20, transcendentals=0
        ),
        name="project",
    )(patches, w_attn)


CHUNK = 256
SPANS = [slice(c * CHUNK, (c + 1) * CHUNK) for c in range(PATCHES // CHUNK)]


def attend_kernel(qkv_ref, out_ref, k_s, v_s, s_s):
    for j, span in enumerate(SPANS):
        k_s[span, :] = qkv_ref[j, 64:128, :].T
        v_s[0:64, span] = qkv_ref[j, 128:192, :]
    v_s[64:80, :] = jnp.ones((16, PATCHES), BF16)

    def scores_of(q_t, span, now):
        scores = dot(k_s[span, :], q_t)
        s_s[now, span, :] = scores
        return jnp.max(scores, axis=0, keepdims=True)

    def weigh(span, before, top):
        probs = jnp.exp2((s_s[before, span, :] - top).astype(BF16))
        return dot(v_s[:, span], probs)

    def finish(block, total):
        out_ref[block] = (total[0:64] / total[64:65]).astype(BF16)

    def both(block, now, top):
        q_t = qkv_ref[block, 0:64, :]
        total = jnp.zeros((80, ROWS), F32)
        tops = []
        for span in SPANS:
            tops.append(scores_of(q_t, span, now))
            total = total + weigh(span, 1 - now, top)
        finish(block - 1, total)
        return functools.reduce(jnp.maximum, tops)

    def pair(t, top):
        top = both(2 * t + 1, 1, top)
        return both(2 * t + 2, 0, top)

    q_t = qkv_ref[0, 0:64, :]
    top = functools.reduce(jnp.maximum, [scores_of(q_t, span, 0) for span in SPANS])
    top = lax.fori_loop(0, 7, pair, top)
    top = both(15, 1, top)
    total = jnp.zeros((80, ROWS), F32)
    for span in SPANS:
        total = total + weigh(span, 1, top)
    finish(15, total)


def attend(qkv):
    return pl.pallas_call(
        attend_kernel,
        out_shape=jax.ShapeDtypeStruct((HEADS, HEAD_DIM, ROWS), BF16),
        in_specs=[RESIDENT],
        out_specs=RESIDENT,
        scratch_shapes=[
            pltpu.VMEM((PATCHES, HEAD_DIM), BF16),
            pltpu.VMEM((80, PATCHES), BF16),
            pltpu.VMEM((2, PATCHES, ROWS), F32),
        ],
        compiler_params=pltpu.CompilerParams(vmem_limit_bytes=VMEM_LIMIT),
        cost_estimate=pl.CostEstimate(
            flops=16 * PATCHES * PATCHES * HEAD_DIM, bytes_accessed=2**21, transcendentals=PATCHES**2
        ),
        name="attend",
    )(qkv)


def self_terms(query, cls_bf16, wk, wv, mask):
    self_key = dot(cls_bf16, wk)
    self_value = dot(cls_bf16, wv)
    product = jnp.where(mask, query * self_key, 0.0)
    score = jnp.sum(product, axis=1, keepdims=True) * LOG2E
    return to_tile(self_value), to_tile(spread(score, mask))


def class_query(cls_bf16, wq):
    return (dot(cls_bf16, wq) * 0.125).astype(BF16).astype(F32)


def start_copies(copies):
    copies = [pltpu.make_async_copy(*copy) for copy in copies]
    for copy in copies:
        copy.start()
    return copies


PIECES = 4
PIECE = D // PIECES


def stream(w_hbm, w_s, sems):
    cut = [slice(PIECE * p, PIECE * (p + 1)) for p in range(PIECES)]
    return start_copies([(w_hbm.at[c], w_s.at[c], sems.at[p]) for p, c in enumerate(cut)])


def dot_streamed(a, w_s, copies):
    total = None
    for p, copy in enumerate(copies):
        cut = slice(PIECE * p, PIECE * (p + 1))
        copy.wait()
        part = dot(a[:, cut], w_s[cut, :])
        total = part if total is None else total + part
    return total


def ahead_kernel(cls_ref, w_hbm, t_ref, self_ref, wq_s, wk_s, wv_s, sems):
    copies = start_copies([(w_hbm.at[0, k], ref, sems.at[k]) for k, ref in enumerate((wq_s, wk_s, wv_s))])
    mask = head_mask()
    cls_bf16 = cls_ref[...].astype(BF16)
    copies[0].wait()
    query = class_query(cls_bf16, wq_s[...])
    spread_query = jnp.where(mask, query, 0.0).astype(BF16)
    copies[1].wait()
    turned = dot(spread_query, wk_s[...], NT) * LOG2E
    t_ref[...] = split_rows(turned)
    copies[2].wait()
    value, score = self_terms(query, cls_bf16, wk_s[...], wv_s[...], mask)
    self_ref[0:8, :] = value
    self_ref[8:16, :] = score


def ahead(cls_in, w_class):
    shapes = (jax.ShapeDtypeStruct((2 * HEADS, D), BF16), jax.ShapeDtypeStruct((16, 128), F32))
    scratch = (SQUARE, SQUARE, SQUARE, pltpu.SemaphoreType.DMA((3,)))
    return call(ahead_kernel, "ahead", 2**30, shapes, (cls_in,), (w_class,), scratch)


def partial_out(scores, values, mask, out_ref):
    top = jnp.max(scores, axis=1, keepdims=True)
    terms = jnp.exp2(scores - top)
    total = jnp.sum(terms, axis=1, keepdims=True)
    weighted = fold_halves(dot(split_rows(terms), values)) / total
    row = jnp.sum(jnp.where(mask, weighted, 0.0), axis=0, keepdims=True)
    tile = jnp.concatenate([to_tile(row), to_tile(spread(top + jnp.log2(total), mask))], axis=0)
    for d in range(HEADS):
        out_ref[d] = tile


def combine(parts_ref, self_ref):
    top = self_ref[8:16, :]
    for d in range(HEADS):
        top = jnp.maximum(top, parts_ref[d, 8:16, :])
    weight = jnp.exp2(self_ref[8:16, :] - top)
    total = weight
    value = weight * self_ref[0:8, :]
    for d in range(HEADS):
        weight = jnp.exp2(parts_ref[d, 8:16, :] - top)
        total = total + weight
        value = value + weight * parts_ref[d, 0:8, :]
    return to_row(value / total).astype(BF16)


def update_kernel(ret_ref, x_ref, t_ref, wo_ref, w_hbm, upd_hbm, part_ref, upd_s, wv_s, sems):
    (weight_copy,) = start_copies([(w_hbm.at[0, 2], wv_s, sems.at[0])])
    mask = head_mask()
    attended = ret_ref[...].reshape(D, ROWS)
    updated = (x_ref[...].astype(F32) + dot(attended, wo_ref[...], TN)).astype(BF16)
    upd_s[...] = updated
    (out_copy,) = start_copies([(upd_s, upd_hbm, sems.at[1])])
    scores = fold_halves(dot(t_ref[...], updated, NT))
    weight_copy.wait()
    values = dot(updated, wv_s[...]).astype(BF16)
    partial_out(scores, values, mask, part_ref)
    out_copy.wait()


def update(returned, patches, w_out, turned, w_class):
    shapes = (
        jax.ShapeDtypeStruct((ROWS, D), BF16),
        jax.ShapeDtypeStruct((HEADS, 16, 128), F32),
    )
    scratch = (pltpu.VMEM((ROWS, D), BF16), SQUARE, pltpu.SemaphoreType.DMA((2,)))
    args = (returned, patches, turned, w_out)
    return call(update_kernel, "update", 4 * ROWS * D * D, shapes, args, (w_class,), scratch, 1)


def class_kv_kernel(upd_hbm, w_hbm, k_ref, v_ref, wo_ref, upd_s, wk_s, wv_s, sems):
    copies = start_copies(
        [
            (upd_hbm, upd_s, sems.at[0]),
            (w_hbm.at[1, 1], wk_s, sems.at[1]),
            (w_hbm.at[1, 2], wv_s, sems.at[2]),
            (w_hbm.at[0, 3], wo_ref, sems.at[3]),
        ]
    )
    copies[0].wait()
    updated = upd_s[...]
    copies[1].wait()
    k_ref[...] = dot(updated, wk_s[...]).astype(BF16)
    copies[2].wait()
    v_ref[...] = dot(updated, wv_s[...]).astype(BF16)
    copies[3].wait()


def class_kv(updated, w_class):
    rows = jax.ShapeDtypeStruct((ROWS, D), BF16)
    shapes = (rows, rows, jax.ShapeDtypeStruct((D, D), BF16))
    scratch = (pltpu.VMEM((ROWS, D), BF16), SQUARE, SQUARE, pltpu.SemaphoreType.DMA((4,)))
    return call(class_kv_kernel, "class_kv", 2**31, shapes, (), (updated, w_class), scratch)


def middle_kernel(
    parts_ref, self_ref, cls_ref, wo_ref, k_ref, v_ref, w_hbm, cls_out_ref, q_ref, part_ref, wq_s, sems
):
    wq_copies = stream(w_hbm.at[1, 0], wq_s, sems)
    mask = head_mask()
    attn = combine(parts_ref, self_ref)
    cls_token = cls_ref[...] + dot(attn, wo_ref[...])
    cls_out_ref[...] = cls_token
    query = (dot_streamed(cls_token.astype(BF16), wq_s, wq_copies) * 0.125).astype(BF16).astype(F32)
    q_ref[...] = query
    spread_query = jnp.where(mask, query, 0.0).astype(BF16)
    scores = dot(spread_query, k_ref[...], NT) * LOG2E
    partial_out(scores, v_ref[...], mask, part_ref)


def middle(parts, self_part, cls_in, w_o, keys, values, w_class):
    shapes = (
        jax.ShapeDtypeStruct((1, D), F32),
        jax.ShapeDtypeStruct((1, D), F32),
        jax.ShapeDtypeStruct((HEADS, 16, 128), F32),
    )
    args = (parts, self_part, cls_in, w_o, keys, values)
    scratch = (SQUARE, pltpu.SemaphoreType.DMA((PIECES,)))
    return call(middle_kernel, "middle", 2**28, shapes, args, (w_class,), scratch)


def self_kernel(cls_ref, q_ref, w_hbm, self_ref, wo_ref, wk_s, wv_s, sems):
    copies = start_copies(
        [
            (w_hbm.at[1, 1], wk_s, sems.at[0]),
            (w_hbm.at[1, 2], wv_s, sems.at[1]),
            (w_hbm.at[1, 3], wo_ref, sems.at[2]),
        ]
    )
    cls_bf16 = cls_ref[...].astype(BF16)
    copies[0].wait()
    copies[1].wait()
    value, score = self_terms(q_ref[...], cls_bf16, wk_s[...], wv_s[...], head_mask())
    self_ref[0:8, :] = value
    self_ref[8:16, :] = score
    copies[2].wait()


def self_part(cls_token, query, w_class):
    shapes = (jax.ShapeDtypeStruct((16, 128), F32), jax.ShapeDtypeStruct((D, D), BF16))
    scratch = (SQUARE, SQUARE, pltpu.SemaphoreType.DMA((3,)))
    return call(self_kernel, "self_part", 2**30, shapes, (cls_token, query), (w_class,), scratch)


def last_kernel(parts_ref, self_ref, cls_ref, wo_ref, out_ref):
    attn = combine(parts_ref, self_ref)
    out_ref[...] = cls_ref[...] + dot(attn, wo_ref[...])


def last(parts, self_terms_1, cls_token, w_o):
    shape = jax.ShapeDtypeStruct((1, D), F32)
    return call(last_kernel, "last", 2**27, shape, (parts, self_terms_1, cls_token, w_o))


def exchange(blocks):
    return lax.all_to_all(blocks, "patch", 0, 0)


def per_device(patches, cls_in, w_attn, w_out, w_class):
    qkv = exchange(project(patches, w_attn))
    turned, self_0 = ahead(cls_in, w_class)
    returned = exchange(attend(qkv))
    updated, part_0 = update(returned, patches, w_out, turned, w_class)
    parts_0 = exchange(part_0)
    keys, values, w_o_0 = class_kv(updated, w_class)
    cls_1, query_1, part_1 = middle(parts_0, self_0, cls_in, w_o_0, keys, values, w_class)
    parts_1 = exchange(part_1)
    self_1, w_o_1 = self_part(cls_1, query_1, w_class)
    return (updated, last(parts_1, self_1, cls_1, w_o_1))


def solution(mesh):
    placed = (P(("dp", "patch"), None), P("dp", None), P(), P(), P())
    return jax.shard_map(
        per_device,
        mesh=mesh,
        in_specs=placed,
        out_specs=(P(("dp", "patch"), None), P("dp", None)),
        check_vma=False,
    )
```

```python
import functools

import jax
import jax.numpy as jnp
from jax import lax
from jax.experimental import pallas as pl
from jax.experimental.pallas import tpu as pltpu
from jax.sharding import PartitionSpec as P

HEADS = 16
HEAD_DIM = 64
D = 1024
ROWS = 256
PATCHES = 4096
LOG2E = 1.4426950408889634
BF16 = jnp.bfloat16
F32 = jnp.float32
NN = (((1,), (0,)), ((), ()))
NT = (((1,), (1,)), ((), ()))
TN = (((0,), (0,)), ((), ()))
VMEM_LIMIT = 14 * 2**20
SMALL_LIMIT = 8 * 2**20
LARGE_LIMIT = 46 * 2**20


def dot(a, b, dims=NN):
    return lax.dot_general(a, b, dims, preferred_element_type=F32)


RESIDENT = pl.BlockSpec(memory_space=pltpu.VMEM)
ANYWHERE = pl.BlockSpec(memory_space=pl.ANY)


def call(kernel, name, flops, out_shape, resident, remote=(), scratch=(), hbm_out=0):
    single = not isinstance(out_shape, tuple)
    count = 1 if single else len(out_shape)
    out_specs = (ANYWHERE,) * hbm_out + (RESIDENT,) * (count - hbm_out)
    return pl.pallas_call(
        kernel,
        out_shape=out_shape,
        in_specs=[RESIDENT] * len(resident) + [ANYWHERE] * len(remote),
        out_specs=out_specs[0] if single else out_specs,
        scratch_shapes=scratch,
        compiler_params=pltpu.CompilerParams(
            vmem_limit_bytes=LARGE_LIMIT if remote else SMALL_LIMIT
        ),
        cost_estimate=pl.CostEstimate(flops=flops, bytes_accessed=2**20, transcendentals=0),
        name=name,
    )(*resident, *remote)


SQUARE = pltpu.VMEM((D, D), BF16)


def head_mask():
    row = lax.broadcasted_iota(jnp.int32, (HEADS, D), 0)
    lane = lax.broadcasted_iota(jnp.int32, (HEADS, D), 1)
    return lane // HEAD_DIM == row


def split_rows(value):
    high = value.astype(BF16)
    low = (value - high.astype(F32)).astype(BF16)
    return jnp.concatenate([high, low], axis=0)


def fold_halves(value):
    return value[:HEADS] + value[HEADS:]


def spread(column, mask):
    return jnp.sum(jnp.where(mask, column, 0.0), axis=0, keepdims=True)


def to_tile(row):
    return jnp.concatenate([row[:, 128 * j : 128 * (j + 1)] for j in range(8)], axis=0)


def to_row(tile):
    return jnp.concatenate([tile[j : j + 1, :] for j in range(8)], axis=1)


PARTS = ((0, 0, 16), (1, 0, 16), (2, 0, 8), (2, 8, 8))


def project_kernel(x_hbm, w_hbm, out_hbm, x_s, w_s, out_s, x_sem, in_sems, out_sems):
    x_copy = pltpu.make_async_copy(x_hbm, x_s, x_sem)
    x_copy.start()
    copies = []
    for p, (kind, head, count) in enumerate(PARTS):
        cols = slice(head * HEAD_DIM, (head + count) * HEAD_DIM)
        copies.append(
            pltpu.make_async_copy(w_hbm.at[kind, :, cols], w_s.at[kind, :, cols], in_sems.at[p])
        )
        copies[-1].start()
    x_copy.wait()
    x = x_s[...]
    outs = []
    for p, (kind, head, count) in enumerate(PARTS):
        copies[p].wait()
        y = dot(x, w_s[kind, :, head * HEAD_DIM : (head + count) * HEAD_DIM])
        if kind == 0:
            y = y * (0.125 * LOG2E)
        yt = y.astype(BF16).T
        rows = slice(kind * HEAD_DIM, (kind + 1) * HEAD_DIM)
        for h in range(count):
            out_s[head + h, rows, :] = yt[h * HEAD_DIM : (h + 1) * HEAD_DIM]
        heads = slice(head, head + count)
        outs.append(
            pltpu.make_async_copy(
                out_s.at[heads, rows, :], out_hbm.at[heads, rows, :], out_sems.at[p]
            )
        )
        outs[-1].start()
    for copy in outs:
        copy.wait()


def project(patches, w_attn):
    packed = (HEADS, 3 * HEAD_DIM, ROWS)
    return pl.pallas_call(
        project_kernel,
        out_shape=jax.ShapeDtypeStruct(packed, BF16),
        in_specs=[ANYWHERE] * 2,
        out_specs=ANYWHERE,
        scratch_shapes=[
            pltpu.VMEM((ROWS, D), BF16),
            pltpu.VMEM((3, D, D), BF16),
            pltpu.VMEM(packed, BF16),
            pltpu.SemaphoreType.DMA(()),
            pltpu.SemaphoreType.DMA((len(PARTS),)),
            pltpu.SemaphoreType.DMA((len(PARTS),)),
        ],
        compiler_params=pltpu.CompilerParams(vmem_limit_bytes=62 * 2**20),
        cost_estimate=pl.CostEstimate(
            flops=2 * ROWS * D * 3 * D, bytes_accessed=8 * 2**20, transcendentals=0
        ),
        name="project",
    )(patches, w_attn)


CHUNK = 256
SPANS = [slice(c * CHUNK, (c + 1) * CHUNK) for c in range(PATCHES // CHUNK)]


def attend_kernel(qkv_ref, out_ref, k_s, v_s, s_s):
    for j, span in enumerate(SPANS):
        k_s[span, :] = qkv_ref[j, 64:128, :].T
        v_s[0:64, span] = qkv_ref[j, 128:192, :]
    v_s[64:80, :] = jnp.ones((16, PATCHES), BF16)

    def scores_of(q_t, span, now):
        scores = dot(k_s[span, :], q_t)
        s_s[now, span, :] = scores
        return jnp.max(scores, axis=0, keepdims=True)

    def weigh(span, before, top):
        probs = jnp.exp2(s_s[before, span, :] - top).astype(BF16)
        return dot(v_s[:, span], probs)

    def finish(block, total):
        out_ref[block] = (total[0:64] / total[64:65]).astype(BF16)

    def both(block, now, top):
        q_t = qkv_ref[block, 0:64, :]
        total = jnp.zeros((80, ROWS), F32)
        tops = []
        for span in SPANS:
            tops.append(scores_of(q_t, span, now))
            total = total + weigh(span, 1 - now, top)
        finish(block - 1, total)
        return functools.reduce(jnp.maximum, tops)

    def pair(t, top):
        top = both(2 * t + 1, 1, top)
        return both(2 * t + 2, 0, top)

    q_t = qkv_ref[0, 0:64, :]
    top = functools.reduce(jnp.maximum, [scores_of(q_t, span, 0) for span in SPANS])
    top = lax.fori_loop(0, 7, pair, top)
    top = both(15, 1, top)
    total = jnp.zeros((80, ROWS), F32)
    for span in SPANS:
        total = total + weigh(span, 1, top)
    finish(15, total)


def attend(qkv):
    return pl.pallas_call(
        attend_kernel,
        out_shape=jax.ShapeDtypeStruct((HEADS, HEAD_DIM, ROWS), BF16),
        in_specs=[RESIDENT],
        out_specs=RESIDENT,
        scratch_shapes=[
            pltpu.VMEM((PATCHES, HEAD_DIM), BF16),
            pltpu.VMEM((80, PATCHES), BF16),
            pltpu.VMEM((2, PATCHES, ROWS), F32),
        ],
        compiler_params=pltpu.CompilerParams(vmem_limit_bytes=VMEM_LIMIT),
        cost_estimate=pl.CostEstimate(
            flops=16 * PATCHES * PATCHES * HEAD_DIM, bytes_accessed=2**21, transcendentals=PATCHES**2
        ),
        name="attend",
    )(qkv)


def self_terms(query, cls_bf16, wk, wv, mask):
    self_key = dot(cls_bf16, wk)
    self_value = dot(cls_bf16, wv)
    product = jnp.where(mask, query * self_key, 0.0)
    score = jnp.sum(product, axis=1, keepdims=True) * LOG2E
    return to_tile(self_value), to_tile(spread(score, mask))


def class_query(cls_bf16, wq):
    return (dot(cls_bf16, wq) * 0.125).astype(BF16).astype(F32)


def start_copies(copies):
    copies = [pltpu.make_async_copy(*copy) for copy in copies]
    for copy in copies:
        copy.start()
    return copies


PIECES = 4
PIECE = D // PIECES


def stream(w_hbm, w_s, sems):
    cut = [slice(PIECE * p, PIECE * (p + 1)) for p in range(PIECES)]
    return start_copies([(w_hbm.at[c], w_s.at[c], sems.at[p]) for p, c in enumerate(cut)])


def dot_streamed(a, w_s, copies):
    total = None
    for p, copy in enumerate(copies):
        cut = slice(PIECE * p, PIECE * (p + 1))
        copy.wait()
        part = dot(a[:, cut], w_s[cut, :])
        total = part if total is None else total + part
    return total


def ahead_kernel(cls_ref, w_hbm, t_ref, self_ref, wq_s, wk_s, wv_s, sems):
    copies = start_copies([(w_hbm.at[0, k], ref, sems.at[k]) for k, ref in enumerate((wq_s, wk_s, wv_s))])
    mask = head_mask()
    cls_bf16 = cls_ref[...].astype(BF16)
    copies[0].wait()
    query = class_query(cls_bf16, wq_s[...])
    spread_query = jnp.where(mask, query, 0.0).astype(BF16)
    copies[1].wait()
    turned = dot(spread_query, wk_s[...], NT) * LOG2E
    t_ref[...] = split_rows(turned)
    copies[2].wait()
    value, score = self_terms(query, cls_bf16, wk_s[...], wv_s[...], mask)
    self_ref[0:8, :] = value
    self_ref[8:16, :] = score


def ahead(cls_in, w_class):
    shapes = (jax.ShapeDtypeStruct((2 * HEADS, D), BF16), jax.ShapeDtypeStruct((16, 128), F32))
    scratch = (SQUARE, SQUARE, SQUARE, pltpu.SemaphoreType.DMA((3,)))
    return call(ahead_kernel, "ahead", 2**30, shapes, (cls_in,), (w_class,), scratch)


def partial_out(scores, values, mask, out_ref):
    top = jnp.max(scores, axis=1, keepdims=True)
    terms = jnp.exp2(scores - top)
    total = jnp.sum(terms, axis=1, keepdims=True)
    weighted = fold_halves(dot(split_rows(terms), values)) / total
    row = jnp.sum(jnp.where(mask, weighted, 0.0), axis=0, keepdims=True)
    tile = jnp.concatenate([to_tile(row), to_tile(spread(top + jnp.log2(total), mask))], axis=0)
    for d in range(HEADS):
        out_ref[d] = tile


def combine(parts_ref, self_ref):
    top = self_ref[8:16, :]
    for d in range(HEADS):
        top = jnp.maximum(top, parts_ref[d, 8:16, :])
    weight = jnp.exp2(self_ref[8:16, :] - top)
    total = weight
    value = weight * self_ref[0:8, :]
    for d in range(HEADS):
        weight = jnp.exp2(parts_ref[d, 8:16, :] - top)
        total = total + weight
        value = value + weight * parts_ref[d, 0:8, :]
    return to_row(value / total).astype(BF16)


def update_kernel(ret_ref, x_ref, t_ref, wo_ref, w_hbm, upd_hbm, part_ref, upd_s, wv_s, sems):
    (weight_copy,) = start_copies([(w_hbm.at[0, 2], wv_s, sems.at[0])])
    mask = head_mask()
    attended = ret_ref[...].reshape(D, ROWS)
    updated = (x_ref[...].astype(F32) + dot(attended, wo_ref[...], TN)).astype(BF16)
    upd_s[...] = updated
    (out_copy,) = start_copies([(upd_s, upd_hbm, sems.at[1])])
    scores = fold_halves(dot(t_ref[...], updated, NT))
    weight_copy.wait()
    values = dot(updated, wv_s[...]).astype(BF16)
    partial_out(scores, values, mask, part_ref)
    out_copy.wait()


def update(returned, patches, w_out, turned, w_class):
    shapes = (
        jax.ShapeDtypeStruct((ROWS, D), BF16),
        jax.ShapeDtypeStruct((HEADS, 16, 128), F32),
    )
    scratch = (pltpu.VMEM((ROWS, D), BF16), SQUARE, pltpu.SemaphoreType.DMA((2,)))
    args = (returned, patches, turned, w_out)
    return call(update_kernel, "update", 4 * ROWS * D * D, shapes, args, (w_class,), scratch, 1)


def class_kv_kernel(upd_hbm, w_hbm, k_ref, v_ref, wo_ref, upd_s, wk_s, wv_s, sems):
    copies = start_copies(
        [
            (upd_hbm, upd_s, sems.at[0]),
            (w_hbm.at[1, 1], wk_s, sems.at[1]),
            (w_hbm.at[1, 2], wv_s, sems.at[2]),
            (w_hbm.at[0, 3], wo_ref, sems.at[3]),
        ]
    )
    copies[0].wait()
    updated = upd_s[...]
    copies[1].wait()
    k_ref[...] = dot(updated, wk_s[...]).astype(BF16)
    copies[2].wait()
    v_ref[...] = dot(updated, wv_s[...]).astype(BF16)
    copies[3].wait()


def class_kv(updated, w_class):
    rows = jax.ShapeDtypeStruct((ROWS, D), BF16)
    shapes = (rows, rows, jax.ShapeDtypeStruct((D, D), BF16))
    scratch = (pltpu.VMEM((ROWS, D), BF16), SQUARE, SQUARE, pltpu.SemaphoreType.DMA((4,)))
    return call(class_kv_kernel, "class_kv", 2**31, shapes, (), (updated, w_class), scratch)


def middle_kernel(
    parts_ref, self_ref, cls_ref, wo_ref, k_ref, v_ref, w_hbm, cls_out_ref, q_ref, part_ref, wq_s, sems
):
    wq_copies = stream(w_hbm.at[1, 0], wq_s, sems)
    mask = head_mask()
    attn = combine(parts_ref, self_ref)
    cls_token = cls_ref[...] + dot(attn, wo_ref[...])
    cls_out_ref[...] = cls_token
    query = (dot_streamed(cls_token.astype(BF16), wq_s, wq_copies) * 0.125).astype(BF16).astype(F32)
    q_ref[...] = query
    spread_query = jnp.where(mask, query, 0.0).astype(BF16)
    scores = dot(spread_query, k_ref[...], NT) * LOG2E
    partial_out(scores, v_ref[...], mask, part_ref)


def middle(parts, self_part, cls_in, w_o, keys, values, w_class):
    shapes = (
        jax.ShapeDtypeStruct((1, D), F32),
        jax.ShapeDtypeStruct((1, D), F32),
        jax.ShapeDtypeStruct((HEADS, 16, 128), F32),
    )
    args = (parts, self_part, cls_in, w_o, keys, values)
    scratch = (SQUARE, pltpu.SemaphoreType.DMA((PIECES,)))
    return call(middle_kernel, "middle", 2**28, shapes, args, (w_class,), scratch)


def self_kernel(cls_ref, q_ref, w_hbm, self_ref, wo_ref, wk_s, wv_s, sems):
    copies = start_copies(
        [
            (w_hbm.at[1, 1], wk_s, sems.at[0]),
            (w_hbm.at[1, 2], wv_s, sems.at[1]),
            (w_hbm.at[1, 3], wo_ref, sems.at[2]),
        ]
    )
    cls_bf16 = cls_ref[...].astype(BF16)
    copies[0].wait()
    copies[1].wait()
    value, score = self_terms(q_ref[...], cls_bf16, wk_s[...], wv_s[...], head_mask())
    self_ref[0:8, :] = value
    self_ref[8:16, :] = score
    copies[2].wait()


def self_part(cls_token, query, w_class):
    shapes = (jax.ShapeDtypeStruct((16, 128), F32), jax.ShapeDtypeStruct((D, D), BF16))
    scratch = (SQUARE, SQUARE, pltpu.SemaphoreType.DMA((3,)))
    return call(self_kernel, "self_part", 2**30, shapes, (cls_token, query), (w_class,), scratch)


def last_kernel(parts_ref, self_ref, cls_ref, wo_ref, out_ref):
    attn = combine(parts_ref, self_ref)
    out_ref[...] = cls_ref[...] + dot(attn, wo_ref[...])


def last(parts, self_terms_1, cls_token, w_o):
    shape = jax.ShapeDtypeStruct((1, D), F32)
    return call(last_kernel, "last", 2**27, shape, (parts, self_terms_1, cls_token, w_o))


def exchange(blocks):
    return lax.all_to_all(blocks, "patch", 0, 0)


def per_device(patches, cls_in, w_attn, w_out, w_class):
    qkv = exchange(project(patches, w_attn))
    turned, self_0 = ahead(cls_in, w_class)
    returned = exchange(attend(qkv))
    updated, part_0 = update(returned, patches, w_out, turned, w_class)
    parts_0 = exchange(part_0)
    keys, values, w_o_0 = class_kv(updated, w_class)
    cls_1, query_1, part_1 = middle(parts_0, self_0, cls_in, w_o_0, keys, values, w_class)
    parts_1 = exchange(part_1)
    self_1, w_o_1 = self_part(cls_1, query_1, w_class)
    return (updated, last(parts_1, self_1, cls_1, w_o_1))


def solution(mesh):
    placed = (P(("dp", "patch"), None), P("dp", None), P(), P(), P())
    return jax.shard_map(
        per_device,
        mesh=mesh,
        in_specs=placed,
        out_specs=(P(("dp", "patch"), None), P("dp", None)),
        check_vma=False,
    )
```

```python
import functools

import jax
import jax.numpy as jnp
from jax import lax
from jax.experimental import pallas as pl
from jax.experimental.pallas import tpu as pltpu
from jax.sharding import PartitionSpec as P

HEADS = 16
HEAD_DIM = 64
D = 1024
ROWS = 256
PATCHES = 4096
LOG2E = 1.4426950408889634
BF16 = jnp.bfloat16
F32 = jnp.float32
NN = (((1,), (0,)), ((), ()))
NT = (((1,), (1,)), ((), ()))
TN = (((0,), (0,)), ((), ()))
VMEM_LIMIT = 14 * 2**20
SMALL_LIMIT = 8 * 2**20
LARGE_LIMIT = 46 * 2**20


def dot(a, b, dims=NN):
    return lax.dot_general(a, b, dims, preferred_element_type=F32)


RESIDENT = pl.BlockSpec(memory_space=pltpu.VMEM)
ANYWHERE = pl.BlockSpec(memory_space=pl.ANY)


def call(kernel, name, flops, out_shape, resident, remote=(), scratch=(), hbm_out=0):
    single = not isinstance(out_shape, tuple)
    count = 1 if single else len(out_shape)
    out_specs = (ANYWHERE,) * hbm_out + (RESIDENT,) * (count - hbm_out)
    return pl.pallas_call(
        kernel,
        out_shape=out_shape,
        in_specs=[RESIDENT] * len(resident) + [ANYWHERE] * len(remote),
        out_specs=out_specs[0] if single else out_specs,
        scratch_shapes=scratch,
        compiler_params=pltpu.CompilerParams(
            vmem_limit_bytes=LARGE_LIMIT if remote else SMALL_LIMIT
        ),
        cost_estimate=pl.CostEstimate(flops=flops, bytes_accessed=2**20, transcendentals=0),
        name=name,
    )(*resident, *remote)


SQUARE = pltpu.VMEM((D, D), BF16)


def head_mask():
    row = lax.broadcasted_iota(jnp.int32, (HEADS, D), 0)
    lane = lax.broadcasted_iota(jnp.int32, (HEADS, D), 1)
    return lane // HEAD_DIM == row


def split_rows(value):
    high = value.astype(BF16)
    low = (value - high.astype(F32)).astype(BF16)
    return jnp.concatenate([high, low], axis=0)


def fold_halves(value):
    return value[:HEADS] + value[HEADS:]


def spread(column, mask):
    return jnp.sum(jnp.where(mask, column, 0.0), axis=0, keepdims=True)


def to_tile(row):
    return jnp.concatenate([row[:, 128 * j : 128 * (j + 1)] for j in range(8)], axis=0)


def to_row(tile):
    return jnp.concatenate([tile[j : j + 1, :] for j in range(8)], axis=1)


def project_kernel(x_ref, w_hbm, out_ref, w_s, w_sem):
    copies = [pltpu.make_async_copy(w_hbm.at[k], w_s.at[k], w_sem.at[k]) for k in range(3)]
    for copy in copies:
        copy.start()
    x = x_ref[...]
    for kind in range(3):
        copies[kind].wait()
        y = dot(x, w_s[kind])
        if kind == 0:
            y = y * (0.125 * LOG2E)
        yt = y.astype(BF16).T
        for h in range(HEADS):
            out_ref[h, kind * HEAD_DIM : (kind + 1) * HEAD_DIM, :] = yt[
                h * HEAD_DIM : (h + 1) * HEAD_DIM
            ]


def project(patches, w_attn):
    return pl.pallas_call(
        project_kernel,
        out_shape=jax.ShapeDtypeStruct((HEADS, 3 * HEAD_DIM, ROWS), BF16),
        in_specs=[RESIDENT, ANYWHERE],
        out_specs=RESIDENT,
        scratch_shapes=[
            pltpu.VMEM((3, D, D), BF16),
            pltpu.SemaphoreType.DMA((3,)),
        ],
        compiler_params=pltpu.CompilerParams(vmem_limit_bytes=50 * 2**20),
        cost_estimate=pl.CostEstimate(
            flops=2 * ROWS * D * 3 * D, bytes_accessed=8 * 2**20, transcendentals=0
        ),
        name="project",
    )(patches, w_attn)


CHUNK = 256
SPANS = [slice(c * CHUNK, (c + 1) * CHUNK) for c in range(PATCHES // CHUNK)]


def attend_kernel(qkv_ref, out_hbm, k_s, v_s, s_s, out_s, sems):
    for j, span in enumerate(SPANS):
        k_s[span, :] = qkv_ref[j, 64:128, :].T
        v_s[0:64, span] = qkv_ref[j, 128:192, :]
    v_s[64:80, :] = jnp.ones((16, PATCHES), BF16)

    def scores_of(q_t, span, now):
        scores = dot(k_s[span, :], q_t)
        s_s[now, span, :] = scores
        return jnp.max(scores, axis=0, keepdims=True)

    def weigh(span, before, top):
        probs = jnp.exp2(s_s[before, span, :] - top).astype(BF16)
        return dot(v_s[:, span], probs)

    def leave(block):
        return pltpu.make_async_copy(out_s.at[block], out_hbm.at[block], sems.at[block])

    def finish(block, total):
        out_s[block] = (total[0:64] / total[64:65]).astype(BF16)
        leave(block).start()

    def both(block, now, top):
        q_t = qkv_ref[block, 0:64, :]
        total = jnp.zeros((80, ROWS), F32)
        tops = []
        for span in SPANS:
            tops.append(scores_of(q_t, span, now))
            total = total + weigh(span, 1 - now, top)
        finish(block - 1, total)
        return functools.reduce(jnp.maximum, tops)

    def pair(t, top):
        top = both(2 * t + 1, 1, top)
        return both(2 * t + 2, 0, top)

    q_t = qkv_ref[0, 0:64, :]
    top = functools.reduce(jnp.maximum, [scores_of(q_t, span, 0) for span in SPANS])
    top = lax.fori_loop(0, 7, pair, top)
    top = both(15, 1, top)
    total = jnp.zeros((80, ROWS), F32)
    for span in SPANS:
        total = total + weigh(span, 1, top)
    finish(15, total)
    for block in range(HEADS):
        leave(block).wait()


def attend(qkv):
    return pl.pallas_call(
        attend_kernel,
        out_shape=jax.ShapeDtypeStruct((HEADS, HEAD_DIM, ROWS), BF16),
        in_specs=[RESIDENT],
        out_specs=ANYWHERE,
        scratch_shapes=[
            pltpu.VMEM((PATCHES, HEAD_DIM), BF16),
            pltpu.VMEM((80, PATCHES), BF16),
            pltpu.VMEM((2, PATCHES, ROWS), F32),
            pltpu.VMEM((HEADS, HEAD_DIM, ROWS), BF16),
            pltpu.SemaphoreType.DMA((HEADS,)),
        ],
        compiler_params=pltpu.CompilerParams(vmem_limit_bytes=VMEM_LIMIT),
        cost_estimate=pl.CostEstimate(
            flops=16 * PATCHES * PATCHES * HEAD_DIM, bytes_accessed=2**21, transcendentals=PATCHES**2
        ),
        name="attend",
    )(qkv)


def self_terms(query, cls_bf16, wk, wv, mask):
    self_key = dot(cls_bf16, wk)
    self_value = dot(cls_bf16, wv)
    product = jnp.where(mask, query * self_key, 0.0)
    score = jnp.sum(product, axis=1, keepdims=True) * LOG2E
    return to_tile(self_value), to_tile(spread(score, mask))


def class_query(cls_bf16, wq):
    return (dot(cls_bf16, wq) * 0.125).astype(BF16).astype(F32)


def start_copies(copies):
    copies = [pltpu.make_async_copy(*copy) for copy in copies]
    for copy in copies:
        copy.start()
    return copies


PIECES = 4
PIECE = D // PIECES


def stream(w_hbm, w_s, sems):
    cut = [slice(PIECE * p, PIECE * (p + 1)) for p in range(PIECES)]
    return start_copies([(w_hbm.at[c], w_s.at[c], sems.at[p]) for p, c in enumerate(cut)])


def dot_streamed(a, w_s, copies):
    total = None
    for p, copy in enumerate(copies):
        cut = slice(PIECE * p, PIECE * (p + 1))
        copy.wait()
        part = dot(a[:, cut], w_s[cut, :])
        total = part if total is None else total + part
    return total


def ahead_kernel(cls_ref, w_hbm, t_ref, self_ref, wq_s, wk_s, wv_s, sems):
    copies = start_copies([(w_hbm.at[0, k], ref, sems.at[k]) for k, ref in enumerate((wq_s, wk_s, wv_s))])
    mask = head_mask()
    cls_bf16 = cls_ref[...].astype(BF16)
    copies[0].wait()
    query = class_query(cls_bf16, wq_s[...])
    spread_query = jnp.where(mask, query, 0.0).astype(BF16)
    copies[1].wait()
    turned = dot(spread_query, wk_s[...], NT) * LOG2E
    t_ref[...] = split_rows(turned)
    copies[2].wait()
    value, score = self_terms(query, cls_bf16, wk_s[...], wv_s[...], mask)
    self_ref[0:8, :] = value
    self_ref[8:16, :] = score


def ahead(cls_in, w_class):
    shapes = (jax.ShapeDtypeStruct((2 * HEADS, D), BF16), jax.ShapeDtypeStruct((16, 128), F32))
    scratch = (SQUARE, SQUARE, SQUARE, pltpu.SemaphoreType.DMA((3,)))
    return call(ahead_kernel, "ahead", 2**30, shapes, (cls_in,), (w_class,), scratch)


def partial_out(scores, values, mask, out_ref):
    top = jnp.max(scores, axis=1, keepdims=True)
    terms = jnp.exp2(scores - top)
    total = jnp.sum(terms, axis=1, keepdims=True)
    weighted = fold_halves(dot(split_rows(terms), values)) / total
    row = jnp.sum(jnp.where(mask, weighted, 0.0), axis=0, keepdims=True)
    tile = jnp.concatenate([to_tile(row), to_tile(spread(top + jnp.log2(total), mask))], axis=0)
    for d in range(HEADS):
        out_ref[d] = tile


def combine(parts_ref, self_ref):
    top = self_ref[8:16, :]
    for d in range(HEADS):
        top = jnp.maximum(top, parts_ref[d, 8:16, :])
    weight = jnp.exp2(self_ref[8:16, :] - top)
    total = weight
    value = weight * self_ref[0:8, :]
    for d in range(HEADS):
        weight = jnp.exp2(parts_ref[d, 8:16, :] - top)
        total = total + weight
        value = value + weight * parts_ref[d, 0:8, :]
    return to_row(value / total).astype(BF16)


def update_kernel(ret_ref, x_ref, t_ref, wo_ref, w_hbm, upd_hbm, part_ref, upd_s, wv_s, sems):
    (weight_copy,) = start_copies([(w_hbm.at[0, 2], wv_s, sems.at[0])])
    mask = head_mask()
    attended = ret_ref[...].reshape(D, ROWS)
    updated = (x_ref[...].astype(F32) + dot(attended, wo_ref[...], TN)).astype(BF16)
    upd_s[...] = updated
    (out_copy,) = start_copies([(upd_s, upd_hbm, sems.at[1])])
    scores = fold_halves(dot(t_ref[...], updated, NT))
    weight_copy.wait()
    values = dot(updated, wv_s[...]).astype(BF16)
    partial_out(scores, values, mask, part_ref)
    out_copy.wait()


def update(returned, patches, w_out, turned, w_class):
    shapes = (
        jax.ShapeDtypeStruct((ROWS, D), BF16),
        jax.ShapeDtypeStruct((HEADS, 16, 128), F32),
    )
    scratch = (pltpu.VMEM((ROWS, D), BF16), SQUARE, pltpu.SemaphoreType.DMA((2,)))
    args = (returned, patches, turned, w_out)
    return call(update_kernel, "update", 4 * ROWS * D * D, shapes, args, (w_class,), scratch, 1)


def class_kv_kernel(upd_hbm, w_hbm, k_ref, v_ref, wo_ref, upd_s, wk_s, wv_s, sems):
    copies = start_copies(
        [
            (upd_hbm, upd_s, sems.at[0]),
            (w_hbm.at[1, 1], wk_s, sems.at[1]),
            (w_hbm.at[1, 2], wv_s, sems.at[2]),
            (w_hbm.at[0, 3], wo_ref, sems.at[3]),
        ]
    )
    copies[0].wait()
    updated = upd_s[...]
    copies[1].wait()
    k_ref[...] = dot(updated, wk_s[...]).astype(BF16)
    copies[2].wait()
    v_ref[...] = dot(updated, wv_s[...]).astype(BF16)
    copies[3].wait()


def class_kv(updated, w_class):
    rows = jax.ShapeDtypeStruct((ROWS, D), BF16)
    shapes = (rows, rows, jax.ShapeDtypeStruct((D, D), BF16))
    scratch = (pltpu.VMEM((ROWS, D), BF16), SQUARE, SQUARE, pltpu.SemaphoreType.DMA((4,)))
    return call(class_kv_kernel, "class_kv", 2**31, shapes, (), (updated, w_class), scratch)


def middle_kernel(
    parts_ref, self_ref, cls_ref, wo_ref, k_ref, v_ref, w_hbm, cls_out_ref, q_ref, part_ref, wq_s, sems
):
    wq_copies = stream(w_hbm.at[1, 0], wq_s, sems)
    mask = head_mask()
    attn = combine(parts_ref, self_ref)
    cls_token = cls_ref[...] + dot(attn, wo_ref[...])
    cls_out_ref[...] = cls_token
    query = (dot_streamed(cls_token.astype(BF16), wq_s, wq_copies) * 0.125).astype(BF16).astype(F32)
    q_ref[...] = query
    spread_query = jnp.where(mask, query, 0.0).astype(BF16)
    scores = dot(spread_query, k_ref[...], NT) * LOG2E
    partial_out(scores, v_ref[...], mask, part_ref)


def middle(parts, self_part, cls_in, w_o, keys, values, w_class):
    shapes = (
        jax.ShapeDtypeStruct((1, D), F32),
        jax.ShapeDtypeStruct((1, D), F32),
        jax.ShapeDtypeStruct((HEADS, 16, 128), F32),
    )
    args = (parts, self_part, cls_in, w_o, keys, values)
    scratch = (SQUARE, pltpu.SemaphoreType.DMA((PIECES,)))
    return call(middle_kernel, "middle", 2**28, shapes, args, (w_class,), scratch)


def self_kernel(cls_ref, q_ref, w_hbm, self_ref, wo_ref, wk_s, wv_s, sems):
    copies = start_copies(
        [
            (w_hbm.at[1, 1], wk_s, sems.at[0]),
            (w_hbm.at[1, 2], wv_s, sems.at[1]),
            (w_hbm.at[1, 3], wo_ref, sems.at[2]),
        ]
    )
    cls_bf16 = cls_ref[...].astype(BF16)
    copies[0].wait()
    copies[1].wait()
    value, score = self_terms(q_ref[...], cls_bf16, wk_s[...], wv_s[...], head_mask())
    self_ref[0:8, :] = value
    self_ref[8:16, :] = score
    copies[2].wait()


def self_part(cls_token, query, w_class):
    shapes = (jax.ShapeDtypeStruct((16, 128), F32), jax.ShapeDtypeStruct((D, D), BF16))
    scratch = (SQUARE, SQUARE, pltpu.SemaphoreType.DMA((3,)))
    return call(self_kernel, "self_part", 2**30, shapes, (cls_token, query), (w_class,), scratch)


def last_kernel(parts_ref, self_ref, cls_ref, wo_ref, out_ref):
    attn = combine(parts_ref, self_ref)
    out_ref[...] = cls_ref[...] + dot(attn, wo_ref[...])


def last(parts, self_terms_1, cls_token, w_o):
    shape = jax.ShapeDtypeStruct((1, D), F32)
    return call(last_kernel, "last", 2**27, shape, (parts, self_terms_1, cls_token, w_o))


def exchange(blocks):
    return lax.all_to_all(blocks, "patch", 0, 0)


def per_device(patches, cls_in, w_attn, w_out, w_class):
    qkv = exchange(project(patches, w_attn))
    turned, self_0 = ahead(cls_in, w_class)
    returned = exchange(attend(qkv))
    updated, part_0 = update(returned, patches, w_out, turned, w_class)
    parts_0 = exchange(part_0)
    keys, values, w_o_0 = class_kv(updated, w_class)
    cls_1, query_1, part_1 = middle(parts_0, self_0, cls_in, w_o_0, keys, values, w_class)
    parts_1 = exchange(part_1)
    self_1, w_o_1 = self_part(cls_1, query_1, w_class)
    return (updated, last(parts_1, self_1, cls_1, w_o_1))


def solution(mesh):
    placed = (P(("dp", "patch"), None), P("dp", None), P(), P(), P())
    return jax.shard_map(
        per_device,
        mesh=mesh,
        in_specs=placed,
        out_specs=(P(("dp", "patch"), None), P("dp", None)),
        check_vma=False,
    )
```

```python
import functools

import jax
import jax.numpy as jnp
from jax import lax
from jax.experimental import pallas as pl
from jax.experimental.pallas import tpu as pltpu
from jax.sharding import PartitionSpec as P

HEADS = 16
HEAD_DIM = 64
D = 1024
ROWS = 256
PATCHES = 4096
LOG2E = 1.4426950408889634
BF16 = jnp.bfloat16
F32 = jnp.float32
NN = (((1,), (0,)), ((), ()))
NT = (((1,), (1,)), ((), ()))
TN = (((0,), (0,)), ((), ()))
VMEM_LIMIT = 14 * 2**20
SMALL_LIMIT = 8 * 2**20
LARGE_LIMIT = 46 * 2**20
PROJECT_LIMIT = 50 * 2**20


def dot(a, b, dims=NN):
    return lax.dot_general(a, b, dims, preferred_element_type=F32)


RESIDENT = pl.BlockSpec(memory_space=pltpu.VMEM)
ANYWHERE = pl.BlockSpec(memory_space=pl.ANY)


def call(kernel, name, flops, out_shape, resident, remote=(), scratch=(), hbm_out=0):
    single = not isinstance(out_shape, tuple)
    count = 1 if single else len(out_shape)
    out_specs = (ANYWHERE,) * hbm_out + (RESIDENT,) * (count - hbm_out)
    return pl.pallas_call(
        kernel,
        out_shape=out_shape,
        in_specs=[RESIDENT] * len(resident) + [ANYWHERE] * len(remote),
        out_specs=out_specs[0] if single else out_specs,
        scratch_shapes=scratch,
        compiler_params=pltpu.CompilerParams(
            vmem_limit_bytes=LARGE_LIMIT if remote else SMALL_LIMIT
        ),
        cost_estimate=pl.CostEstimate(flops=flops, bytes_accessed=2**20, transcendentals=0),
        name=name,
    )(*resident, *remote)


SQUARE = pltpu.VMEM((D, D), BF16)


def head_mask():
    row = lax.broadcasted_iota(jnp.int32, (HEADS, D), 0)
    lane = lax.broadcasted_iota(jnp.int32, (HEADS, D), 1)
    return lane // HEAD_DIM == row


def split_rows(value):
    high = value.astype(BF16)
    low = (value - high.astype(F32)).astype(BF16)
    return jnp.concatenate([high, low], axis=0)


def fold_halves(value):
    return value[:HEADS] + value[HEADS:]


def spread(column, mask):
    return jnp.sum(jnp.where(mask, column, 0.0), axis=0, keepdims=True)


def to_tile(row):
    return jnp.concatenate([row[:, 128 * j : 128 * (j + 1)] for j in range(8)], axis=0)


def to_row(tile):
    return jnp.concatenate([tile[j : j + 1, :] for j in range(8)], axis=1)


def second_core():
    return lax.rem(lax.axis_index("dp"), 2) == 1


def project_kernel(
    x_ref, w_hbm, cls_hbm, class_hbm, out_ref, t_ref, self_ref, base_ref, m_hbm, w_s, m_s, cls_s, sems, sem
):
    copies = start_copies([(w_hbm.at[k], w_s.at[k], sems.at[k]) for k in range(3)])
    x = x_ref[...]
    for kind in range(3):
        copies[kind].wait()
        y = dot(x, w_s[kind])
        if kind == 0:
            y = y * (0.125 * LOG2E)
        yt = y.astype(BF16).T
        for h in range(HEADS):
            out_ref[h, kind * HEAD_DIM : (kind + 1) * HEAD_DIM, :] = yt[
                h * HEAD_DIM : (h + 1) * HEAD_DIM
            ]

    @pl.when(second_core())
    def _():
        (copy,) = start_copies([(cls_hbm, cls_s, sem)])
        copy.wait()
        class_ahead(cls_s[...], class_hbm, t_ref, self_ref, base_ref, m_hbm, w_s, m_s, sems, sem)


AHEAD_SHAPES = (
    jax.ShapeDtypeStruct((2 * HEADS, D), BF16),
    jax.ShapeDtypeStruct((16, 128), F32),
    jax.ShapeDtypeStruct((1, D), F32),
    jax.ShapeDtypeStruct((3, D, D), BF16),
)


def project(patches, w_attn, cls_in, w_class):
    return pl.pallas_call(
        project_kernel,
        out_shape=(jax.ShapeDtypeStruct((HEADS, 3 * HEAD_DIM, ROWS), BF16), *AHEAD_SHAPES),
        in_specs=[RESIDENT, ANYWHERE, ANYWHERE, ANYWHERE],
        out_specs=(RESIDENT, RESIDENT, RESIDENT, RESIDENT, ANYWHERE),
        scratch_shapes=[
            pltpu.VMEM((5, D, D), BF16),
            pltpu.VMEM((D, D), BF16),
            pltpu.VMEM((1, D), F32),
            pltpu.SemaphoreType.DMA((5,)),
            pltpu.SemaphoreType.DMA(()),
        ],
        compiler_params=pltpu.CompilerParams(vmem_limit_bytes=PROJECT_LIMIT),
        cost_estimate=pl.CostEstimate(
            flops=2 * ROWS * D * 3 * D, bytes_accessed=8 * 2**20, transcendentals=0
        ),
        name="project",
    )(patches, w_attn, cls_in, w_class)


CHUNK = 256
SPANS = [slice(c * CHUNK, (c + 1) * CHUNK) for c in range(PATCHES // CHUNK)]


def attend_kernel(qkv_ref, out_hbm, k_s, v_s, s_s, out_s, sems):
    for j, span in enumerate(SPANS):
        k_s[span, :] = qkv_ref[j, 64:128, :].T
        v_s[0:64, span] = qkv_ref[j, 128:192, :]
    v_s[64:80, :] = jnp.ones((16, PATCHES), BF16)

    def scores_of(q_t, span, now):
        scores = dot(k_s[span, :], q_t)
        s_s[now, span, :] = scores
        return jnp.max(scores, axis=0, keepdims=True)

    def weigh(span, before, top):
        probs = jnp.exp2(s_s[before, span, :] - top).astype(BF16)
        return dot(v_s[:, span], probs)

    def leave(block):
        return pltpu.make_async_copy(out_s.at[block], out_hbm.at[block], sems.at[block])

    def finish(block, total):
        out_s[block] = (total[0:64] / total[64:65]).astype(BF16)
        leave(block).start()

    def both(block, now, top):
        q_t = qkv_ref[block, 0:64, :]
        total = jnp.zeros((80, ROWS), F32)
        tops = []
        for span in SPANS:
            tops.append(scores_of(q_t, span, now))
            total = total + weigh(span, 1 - now, top)
        finish(block - 1, total)
        return functools.reduce(jnp.maximum, tops)

    def pair(t, top):
        top = both(2 * t + 1, 1, top)
        return both(2 * t + 2, 0, top)

    q_t = qkv_ref[0, 0:64, :]
    top = functools.reduce(jnp.maximum, [scores_of(q_t, span, 0) for span in SPANS])
    top = lax.fori_loop(0, 7, pair, top)
    top = both(15, 1, top)
    total = jnp.zeros((80, ROWS), F32)
    for span in SPANS:
        total = total + weigh(span, 1, top)
    finish(15, total)
    for block in range(HEADS):
        leave(block).wait()


def attend(qkv):
    return pl.pallas_call(
        attend_kernel,
        out_shape=jax.ShapeDtypeStruct((HEADS, HEAD_DIM, ROWS), BF16),
        in_specs=[RESIDENT],
        out_specs=ANYWHERE,
        scratch_shapes=[
            pltpu.VMEM((PATCHES, HEAD_DIM), BF16),
            pltpu.VMEM((80, PATCHES), BF16),
            pltpu.VMEM((2, PATCHES, ROWS), F32),
            pltpu.VMEM((HEADS, HEAD_DIM, ROWS), BF16),
            pltpu.SemaphoreType.DMA((HEADS,)),
        ],
        compiler_params=pltpu.CompilerParams(vmem_limit_bytes=VMEM_LIMIT),
        cost_estimate=pl.CostEstimate(
            flops=16 * PATCHES * PATCHES * HEAD_DIM, bytes_accessed=2**21, transcendentals=PATCHES**2
        ),
        name="attend",
    )(qkv)


def self_terms(query, cls_bf16, wk, wv, mask):
    self_key = dot(cls_bf16, wk)
    self_value = dot(cls_bf16, wv)
    product = jnp.where(mask, query * self_key, 0.0)
    score = jnp.sum(product, axis=1, keepdims=True) * LOG2E
    return to_tile(self_value), to_tile(spread(score, mask))


def class_query(cls_bf16, wq):
    return (dot(cls_bf16, wq) * 0.125).astype(BF16).astype(F32)


def start_copies(copies):
    copies = [pltpu.make_async_copy(*copy) for copy in copies]
    for copy in copies:
        copy.start()
    return copies


def class_ahead(cls_token, w_hbm, t_ref, self_ref, base_ref, m_hbm, w_s, m_s, sems, sem):
    sources = ((0, 0), (0, 1), (0, 2), (0, 3), (1, 0))
    copies = start_copies([(w_hbm.at[c, k], w_s.at[n], sems.at[n]) for n, (c, k) in enumerate(sources)])
    mask = head_mask()
    cls_bf16 = cls_token.astype(BF16)
    copies[0].wait()
    query = class_query(cls_bf16, w_s[0])
    spread_query = jnp.where(mask, query, 0.0).astype(BF16)
    copies[1].wait()
    turned = dot(spread_query, w_s[1], NT) * LOG2E
    t_ref[...] = split_rows(turned)
    copies[2].wait()
    value, score = self_terms(query, cls_bf16, w_s[1], w_s[2], mask)
    self_ref[0:8, :] = value
    self_ref[8:16, :] = score
    copies[3].wait()
    copies[4].wait()
    low = (cls_token - cls_bf16.astype(F32)).astype(BF16)
    base_ref[...] = dot(cls_bf16, w_s[4]) + dot(low, w_s[4])
    for c in range(4):
        rows = slice(c * 256, (c + 1) * 256)
        m_s[rows, :] = dot(w_s[3, rows, :], w_s[4]).astype(BF16)
    (copy,) = start_copies([(m_s, m_hbm.at[0], sem)])
    copy.wait()


def ahead_kernel(
    cls_ref, t_in, self_in, base_in, w_hbm, m_in, t_ref, self_ref, base_ref, m_hbm, w_s, m_s, sems, sem
):
    del m_in
    second = second_core()

    @pl.when(second)
    def _():
        t_ref[...] = t_in[...]
        self_ref[...] = self_in[...]
        base_ref[...] = base_in[...]

    @pl.when(jnp.logical_not(second))
    def _():
        class_ahead(cls_ref[...], w_hbm, t_ref, self_ref, base_ref, m_hbm, w_s, m_s, sems, sem)


def ahead(cls_in, turned, self_0, base, m, w_class):
    return pl.pallas_call(
        ahead_kernel,
        out_shape=AHEAD_SHAPES,
        in_specs=[RESIDENT] * 4 + [ANYWHERE] * 2,
        out_specs=(RESIDENT, RESIDENT, RESIDENT, ANYWHERE),
        scratch_shapes=[
            pltpu.VMEM((5, D, D), BF16),
            SQUARE,
            pltpu.SemaphoreType.DMA((5,)),
            pltpu.SemaphoreType.DMA(()),
        ],
        input_output_aliases={5: 3},
        compiler_params=pltpu.CompilerParams(vmem_limit_bytes=49 * 2**20),
        cost_estimate=pl.CostEstimate(flops=2**32, bytes_accessed=2**20, transcendentals=0),
        name="ahead",
    )(cls_in, turned, self_0, base, w_class, m)


def partial_out(scores, values, mask, out_ref):
    top = jnp.max(scores, axis=1, keepdims=True)
    terms = jnp.exp2(scores - top)
    total = jnp.sum(terms, axis=1, keepdims=True)
    weighted = fold_halves(dot(split_rows(terms), values)) / total
    row = jnp.sum(jnp.where(mask, weighted, 0.0), axis=0, keepdims=True)
    tile = jnp.concatenate([to_tile(row), to_tile(spread(top + jnp.log2(total), mask))], axis=0)
    for d in range(HEADS):
        out_ref[d] = tile


def combine(parts_ref, self_ref):
    top = self_ref[8:16, :]
    for d in range(HEADS):
        top = jnp.maximum(top, parts_ref[d, 8:16, :])
    weight = jnp.exp2(self_ref[8:16, :] - top)
    total = weight
    value = weight * self_ref[0:8, :]
    for d in range(HEADS):
        weight = jnp.exp2(parts_ref[d, 8:16, :] - top)
        total = total + weight
        value = value + weight * parts_ref[d, 0:8, :]
    return to_row(value / total).astype(BF16)


def update_kernel(ret_ref, x_ref, t_ref, wo_ref, w_hbm, upd_hbm, part_ref, upd_s, wv_s, sems):
    (weight_copy,) = start_copies([(w_hbm.at[0, 2], wv_s, sems.at[0])])
    mask = head_mask()
    attended = ret_ref[...].reshape(D, ROWS)
    updated = (x_ref[...].astype(F32) + dot(attended, wo_ref[...], TN)).astype(BF16)
    upd_s[...] = updated
    (out_copy,) = start_copies([(upd_s, upd_hbm, sems.at[1])])
    scores = fold_halves(dot(t_ref[...], updated, NT))
    weight_copy.wait()
    values = dot(updated, wv_s[...]).astype(BF16)
    partial_out(scores, values, mask, part_ref)
    out_copy.wait()


def update(returned, patches, w_out, turned, w_class):
    shapes = (
        jax.ShapeDtypeStruct((ROWS, D), BF16),
        jax.ShapeDtypeStruct((HEADS, 16, 128), F32),
    )
    scratch = (pltpu.VMEM((ROWS, D), BF16), SQUARE, pltpu.SemaphoreType.DMA((2,)))
    args = (returned, patches, turned, w_out)
    return call(update_kernel, "update", 4 * ROWS * D * D, shapes, args, (w_class,), scratch, 1)


def class_kv_kernel(upd_hbm, w_hbm, m_hbm, k_ref, v_ref, m_ref, upd_s, wk_s, wv_s, sems):
    copies = start_copies(
        [
            (upd_hbm, upd_s, sems.at[0]),
            (w_hbm.at[1, 1], wk_s, sems.at[1]),
            (w_hbm.at[1, 2], wv_s, sems.at[2]),
            (m_hbm.at[0], m_ref, sems.at[3]),
        ]
    )
    copies[0].wait()
    updated = upd_s[...]
    copies[1].wait()
    k_ref[...] = dot(updated, wk_s[...]).astype(BF16)
    copies[2].wait()
    v_ref[...] = dot(updated, wv_s[...]).astype(BF16)
    copies[3].wait()


def class_kv(updated, w_class, m):
    rows = jax.ShapeDtypeStruct((ROWS, D), BF16)
    shapes = (rows, rows, jax.ShapeDtypeStruct((D, D), BF16))
    scratch = (pltpu.VMEM((ROWS, D), BF16), SQUARE, SQUARE, pltpu.SemaphoreType.DMA((4,)))
    return call(class_kv_kernel, "class_kv", 2**31, shapes, (), (updated, w_class, m), scratch)


def middle_kernel(parts_ref, self_ref, base_ref, m_ref, k_ref, v_ref, attn_ref, q_ref, part_ref):
    mask = head_mask()
    attn = combine(parts_ref, self_ref)
    attn_ref[...] = attn.astype(F32)
    query = ((base_ref[...] + dot(attn, m_ref[...])) * 0.125).astype(BF16).astype(F32)
    q_ref[...] = query
    spread_query = jnp.where(mask, query, 0.0).astype(BF16)
    scores = dot(spread_query, k_ref[...], NT) * LOG2E
    partial_out(scores, v_ref[...], mask, part_ref)


def middle(parts, self_part, base, m, keys, values):
    shapes = (
        jax.ShapeDtypeStruct((1, D), F32),
        jax.ShapeDtypeStruct((1, D), F32),
        jax.ShapeDtypeStruct((HEADS, 16, 128), F32),
    )
    return call(middle_kernel, "middle", 2**28, shapes, (parts, self_part, base, m, keys, values))


def self_kernel(cls_ref, attn_ref, q_ref, w_hbm, self_ref, cls_out_ref, wo_ref, w_s, sems):
    copies = start_copies(
        [
            (w_hbm.at[0, 3], w_s.at[0], sems.at[0]),
            (w_hbm.at[1, 1], w_s.at[1], sems.at[1]),
            (w_hbm.at[1, 2], w_s.at[2], sems.at[2]),
            (w_hbm.at[1, 3], wo_ref, sems.at[3]),
        ]
    )
    copies[0].wait()
    cls_token = cls_ref[...] + dot(attn_ref[...].astype(BF16), w_s[0])
    cls_out_ref[...] = cls_token
    copies[1].wait()
    copies[2].wait()
    value, score = self_terms(q_ref[...], cls_token.astype(BF16), w_s[1], w_s[2], head_mask())
    self_ref[0:8, :] = value
    self_ref[8:16, :] = score
    copies[3].wait()


def self_part(cls_in, attn, query, w_class):
    shapes = (
        jax.ShapeDtypeStruct((16, 128), F32),
        jax.ShapeDtypeStruct((1, D), F32),
        jax.ShapeDtypeStruct((D, D), BF16),
    )
    scratch = (pltpu.VMEM((3, D, D), BF16), pltpu.SemaphoreType.DMA((4,)))
    return call(self_kernel, "self_part", 2**30, shapes, (cls_in, attn, query), (w_class,), scratch)


def last_kernel(parts_ref, self_ref, cls_ref, wo_ref, out_ref):
    attn = combine(parts_ref, self_ref)
    out_ref[...] = cls_ref[...] + dot(attn, wo_ref[...])


def last(parts, self_terms_1, cls_token, w_o):
    shape = jax.ShapeDtypeStruct((1, D), F32)
    return call(last_kernel, "last", 2**27, shape, (parts, self_terms_1, cls_token, w_o))


def exchange(blocks):
    return lax.all_to_all(blocks, "patch", 0, 0)


def per_device(patches, cls_in, w_attn, w_out, w_class):
    qkv, turned, self_0, base, m = project(patches, w_attn, cls_in, w_class)
    qkv = exchange(qkv)
    returned = exchange(attend(qkv))
    turned, self_0, base, m = ahead(cls_in, turned, self_0, base, m, w_class)
    updated, part_0 = update(returned, patches, w_out, turned, w_class)
    parts_0 = exchange(part_0)
    keys, values, m = class_kv(updated, w_class, m)
    attn_0, query_1, part_1 = middle(parts_0, self_0, base, m, keys, values)
    parts_1 = exchange(part_1)
    self_1, cls_1, w_o_1 = self_part(cls_in, attn_0, query_1, w_class)
    return (updated, last(parts_1, self_1, cls_1, w_o_1))


def solution(mesh):
    placed = (P(("dp", "patch"), None), P("dp", None), P(), P(), P())
    return jax.shard_map(
        per_device,
        mesh=mesh,
        in_specs=placed,
        out_specs=(P(("dp", "patch"), None), P("dp", None)),
        check_vma=False,
    )
```

```python
import functools

import jax
import jax.numpy as jnp
from jax import lax
from jax.experimental import pallas as pl
from jax.experimental.pallas import tpu as pltpu
from jax.sharding import PartitionSpec as P

HEADS = 16
HEAD_DIM = 64
D = 1024
ROWS = 256
PATCHES = 4096
LOG2E = 1.4426950408889634
BF16 = jnp.bfloat16
F32 = jnp.float32
NN = (((1,), (0,)), ((), ()))
NT = (((1,), (1,)), ((), ()))
TN = (((0,), (0,)), ((), ()))
VMEM_LIMIT = 14 * 2**20
SMALL_LIMIT = 8 * 2**20
LARGE_LIMIT = 46 * 2**20
PROJECT_LIMIT = 62 * 2**20


def dot(a, b, dims=NN):
    return lax.dot_general(a, b, dims, preferred_element_type=F32)


RESIDENT = pl.BlockSpec(memory_space=pltpu.VMEM)
ANYWHERE = pl.BlockSpec(memory_space=pl.ANY)


def call(kernel, name, flops, out_shape, resident, remote=(), scratch=(), hbm_out=0):
    single = not isinstance(out_shape, tuple)
    count = 1 if single else len(out_shape)
    out_specs = (ANYWHERE,) * hbm_out + (RESIDENT,) * (count - hbm_out)
    return pl.pallas_call(
        kernel,
        out_shape=out_shape,
        in_specs=[RESIDENT] * len(resident) + [ANYWHERE] * len(remote),
        out_specs=out_specs[0] if single else out_specs,
        scratch_shapes=scratch,
        compiler_params=pltpu.CompilerParams(
            vmem_limit_bytes=LARGE_LIMIT if remote else SMALL_LIMIT
        ),
        cost_estimate=pl.CostEstimate(flops=flops, bytes_accessed=2**20, transcendentals=0),
        name=name,
    )(*resident, *remote)


SQUARE = pltpu.VMEM((D, D), BF16)


def head_mask():
    row = lax.broadcasted_iota(jnp.int32, (HEADS, D), 0)
    lane = lax.broadcasted_iota(jnp.int32, (HEADS, D), 1)
    return lane // HEAD_DIM == row


def split_rows(value):
    high = value.astype(BF16)
    low = (value - high.astype(F32)).astype(BF16)
    return jnp.concatenate([high, low], axis=0)


def fold_halves(value):
    return value[:HEADS] + value[HEADS:]


def spread(column, mask):
    return jnp.sum(jnp.where(mask, column, 0.0), axis=0, keepdims=True)


def to_tile(row):
    return jnp.concatenate([row[:, 128 * j : 128 * (j + 1)] for j in range(8)], axis=0)


def to_row(tile):
    return jnp.concatenate([tile[j : j + 1, :] for j in range(8)], axis=1)


def second_core():
    return lax.rem(lax.axis_index("dp"), 2) == 1


PARTS = ((0, 0, 16), (1, 0, 16), (2, 0, 8), (2, 8, 8))


def project_kernel(
    x_hbm, w_hbm, cls_hbm, class_hbm, out_hbm, t_ref, self_ref, base_ref, m_hbm,
    w_s, m_s, cls_s, x_s, out_s, sems, sem, out_sems,
):
    def weights(p):
        kind, head, count = PARTS[p]
        cols = slice(head * HEAD_DIM, (head + count) * HEAD_DIM)
        return (w_hbm.at[kind, :, cols], w_s.at[kind, :, cols], sems.at[p])

    x_copy, *copies = start_copies([(x_hbm, x_s, sem), weights(0)])
    x_copy.wait()
    copies += start_copies([weights(1)])
    x = x_s[...]
    outs = []
    for p, (kind, head, count) in enumerate(PARTS):
        copies[p].wait()
        if p == 0:
            copies += start_copies([weights(2), weights(3)])
        y = dot(x, w_s[kind, :, head * HEAD_DIM : (head + count) * HEAD_DIM])
        if kind == 0:
            y = y * (0.125 * LOG2E)
        yt = y.astype(BF16).T
        rows = slice(kind * HEAD_DIM, (kind + 1) * HEAD_DIM)
        for h in range(count):
            out_s[head + h, rows, :] = yt[h * HEAD_DIM : (h + 1) * HEAD_DIM]
        part = slice(head, head + count)
        outs += start_copies([(out_s.at[part, rows, :], out_hbm.at[part, rows, :], out_sems.at[p])])
    for copy in outs:
        copy.wait()

    @pl.when(second_core())
    def _():
        (copy,) = start_copies([(cls_hbm, cls_s, sem)])
        copy.wait()
        class_ahead(cls_s[...], class_hbm, t_ref, self_ref, base_ref, m_hbm, w_s, m_s, sems, sem)


AHEAD_SHAPES = (
    jax.ShapeDtypeStruct((2 * HEADS, D), BF16),
    jax.ShapeDtypeStruct((16, 128), F32),
    jax.ShapeDtypeStruct((1, D), F32),
    jax.ShapeDtypeStruct((3, D, D), BF16),
)


def project(patches, w_attn, cls_in, w_class):
    return pl.pallas_call(
        project_kernel,
        out_shape=(jax.ShapeDtypeStruct((HEADS, 3 * HEAD_DIM, ROWS), BF16), *AHEAD_SHAPES),
        in_specs=[ANYWHERE] * 4,
        out_specs=(ANYWHERE, RESIDENT, RESIDENT, RESIDENT, ANYWHERE),
        scratch_shapes=[
            pltpu.VMEM((5, D, D), BF16),
            pltpu.VMEM((D, D), BF16),
            pltpu.VMEM((1, D), F32),
            pltpu.VMEM((ROWS, D), BF16),
            pltpu.VMEM((HEADS, 3 * HEAD_DIM, ROWS), BF16),
            pltpu.SemaphoreType.DMA((5,)),
            pltpu.SemaphoreType.DMA(()),
            pltpu.SemaphoreType.DMA((len(PARTS),)),
        ],
        compiler_params=pltpu.CompilerParams(vmem_limit_bytes=PROJECT_LIMIT),
        cost_estimate=pl.CostEstimate(
            flops=2 * ROWS * D * 3 * D, bytes_accessed=8 * 2**20, transcendentals=0
        ),
        name="project",
    )(patches, w_attn, cls_in, w_class)


CHUNK = 256
SPANS = [slice(c * CHUNK, (c + 1) * CHUNK) for c in range(PATCHES // CHUNK)]


def attend_kernel(qkv_ref, out_hbm, k_s, v_s, s_s, out_s, sems):
    for j, span in enumerate(SPANS):
        k_s[span, :] = qkv_ref[j, 64:128, :].T
        v_s[0:64, span] = qkv_ref[j, 128:192, :]
    v_s[64:80, :] = jnp.ones((16, PATCHES), BF16)

    def scores_of(q_t, span, now):
        scores = dot(k_s[span, :], q_t)
        s_s[now, span, :] = scores
        return jnp.max(scores, axis=0, keepdims=True)

    def weigh(span, before, top):
        probs = jnp.exp2(s_s[before, span, :] - top).astype(BF16)
        return dot(v_s[:, span], probs)

    def leave(block):
        return pltpu.make_async_copy(out_s.at[block], out_hbm.at[block], sems.at[block])

    def finish(block, total):
        out_s[block] = (total[0:64] / total[64:65]).astype(BF16)
        leave(block).start()

    def both(block, now, top):
        q_t = qkv_ref[block, 0:64, :]
        total = jnp.zeros((80, ROWS), F32)
        tops = []
        for span in SPANS:
            tops.append(scores_of(q_t, span, now))
            total = total + weigh(span, 1 - now, top)
        finish(block - 1, total)
        return functools.reduce(jnp.maximum, tops)

    def pair(t, top):
        top = both(2 * t + 1, 1, top)
        return both(2 * t + 2, 0, top)

    q_t = qkv_ref[0, 0:64, :]
    top = functools.reduce(jnp.maximum, [scores_of(q_t, span, 0) for span in SPANS])
    top = lax.fori_loop(0, 7, pair, top)
    top = both(15, 1, top)
    total = jnp.zeros((80, ROWS), F32)
    for span in SPANS:
        total = total + weigh(span, 1, top)
    finish(15, total)
    for block in range(HEADS):
        leave(block).wait()


def attend(qkv):
    return pl.pallas_call(
        attend_kernel,
        out_shape=jax.ShapeDtypeStruct((HEADS, HEAD_DIM, ROWS), BF16),
        in_specs=[RESIDENT],
        out_specs=ANYWHERE,
        scratch_shapes=[
            pltpu.VMEM((PATCHES, HEAD_DIM), BF16),
            pltpu.VMEM((80, PATCHES), BF16),
            pltpu.VMEM((2, PATCHES, ROWS), F32),
            pltpu.VMEM((HEADS, HEAD_DIM, ROWS), BF16),
            pltpu.SemaphoreType.DMA((HEADS,)),
        ],
        compiler_params=pltpu.CompilerParams(vmem_limit_bytes=VMEM_LIMIT),
        cost_estimate=pl.CostEstimate(
            flops=16 * PATCHES * PATCHES * HEAD_DIM, bytes_accessed=2**21, transcendentals=PATCHES**2
        ),
        name="attend",
    )(qkv)


def self_terms(query, cls_bf16, wk, wv, mask):
    self_key = dot(cls_bf16, wk)
    self_value = dot(cls_bf16, wv)
    product = jnp.where(mask, query * self_key, 0.0)
    score = jnp.sum(product, axis=1, keepdims=True) * LOG2E
    return to_tile(self_value), to_tile(spread(score, mask))


def class_query(cls_bf16, wq):
    return (dot(cls_bf16, wq) * 0.125).astype(BF16).astype(F32)


def start_copies(copies):
    copies = [pltpu.make_async_copy(*copy) for copy in copies]
    for copy in copies:
        copy.start()
    return copies


def class_ahead(cls_token, w_hbm, t_ref, self_ref, base_ref, m_hbm, w_s, m_s, sems, sem):
    sources = ((0, 0), (0, 1), (0, 2), (0, 3), (1, 0))
    copies = start_copies([(w_hbm.at[c, k], w_s.at[n], sems.at[n]) for n, (c, k) in enumerate(sources)])
    mask = head_mask()
    cls_bf16 = cls_token.astype(BF16)
    copies[0].wait()
    query = class_query(cls_bf16, w_s[0])
    spread_query = jnp.where(mask, query, 0.0).astype(BF16)
    copies[1].wait()
    turned = dot(spread_query, w_s[1], NT) * LOG2E
    t_ref[...] = split_rows(turned)
    copies[2].wait()
    value, score = self_terms(query, cls_bf16, w_s[1], w_s[2], mask)
    self_ref[0:8, :] = value
    self_ref[8:16, :] = score
    copies[3].wait()
    copies[4].wait()
    low = (cls_token - cls_bf16.astype(F32)).astype(BF16)
    base_ref[...] = dot(cls_bf16, w_s[4]) + dot(low, w_s[4])
    for c in range(4):
        rows = slice(c * 256, (c + 1) * 256)
        m_s[rows, :] = dot(w_s[3, rows, :], w_s[4]).astype(BF16)
    (copy,) = start_copies([(m_s, m_hbm.at[0], sem)])
    copy.wait()


def ahead_kernel(
    cls_ref, t_in, self_in, base_in, w_hbm, m_in, t_ref, self_ref, base_ref, m_hbm, w_s, m_s, sems, sem
):
    del m_in
    second = second_core()

    @pl.when(second)
    def _():
        t_ref[...] = t_in[...]
        self_ref[...] = self_in[...]
        base_ref[...] = base_in[...]

    @pl.when(jnp.logical_not(second))
    def _():
        class_ahead(cls_ref[...], w_hbm, t_ref, self_ref, base_ref, m_hbm, w_s, m_s, sems, sem)


def ahead(cls_in, turned, self_0, base, m, w_class):
    return pl.pallas_call(
        ahead_kernel,
        out_shape=AHEAD_SHAPES,
        in_specs=[RESIDENT] * 4 + [ANYWHERE] * 2,
        out_specs=(RESIDENT, RESIDENT, RESIDENT, ANYWHERE),
        scratch_shapes=[
            pltpu.VMEM((5, D, D), BF16),
            SQUARE,
            pltpu.SemaphoreType.DMA((5,)),
            pltpu.SemaphoreType.DMA(()),
        ],
        input_output_aliases={5: 3},
        compiler_params=pltpu.CompilerParams(vmem_limit_bytes=49 * 2**20),
        cost_estimate=pl.CostEstimate(flops=2**32, bytes_accessed=2**20, transcendentals=0),
        name="ahead",
    )(cls_in, turned, self_0, base, w_class, m)


def partial_out(scores, values, mask, out_ref):
    top = jnp.max(scores, axis=1, keepdims=True)
    terms = jnp.exp2(scores - top)
    total = jnp.sum(terms, axis=1, keepdims=True)
    weighted = fold_halves(dot(split_rows(terms), values)) / total
    row = jnp.sum(jnp.where(mask, weighted, 0.0), axis=0, keepdims=True)
    tile = jnp.concatenate([to_tile(row), to_tile(spread(top + jnp.log2(total), mask))], axis=0)
    for d in range(HEADS):
        out_ref[d] = tile


def combine(parts_ref, self_ref):
    top = self_ref[8:16, :]
    for d in range(HEADS):
        top = jnp.maximum(top, parts_ref[d, 8:16, :])
    weight = jnp.exp2(self_ref[8:16, :] - top)
    total = weight
    value = weight * self_ref[0:8, :]
    for d in range(HEADS):
        weight = jnp.exp2(parts_ref[d, 8:16, :] - top)
        total = total + weight
        value = value + weight * parts_ref[d, 0:8, :]
    return to_row(value / total).astype(BF16)


def update_kernel(ret_ref, x_ref, t_ref, wo_ref, w_hbm, upd_hbm, part_ref, upd_s, wv_s, sems):
    (weight_copy,) = start_copies([(w_hbm.at[0, 2], wv_s, sems.at[0])])
    mask = head_mask()
    attended = ret_ref[...].reshape(D, ROWS)
    updated = (x_ref[...].astype(F32) + dot(attended, wo_ref[...], TN)).astype(BF16)
    upd_s[...] = updated
    (out_copy,) = start_copies([(upd_s, upd_hbm, sems.at[1])])
    scores = fold_halves(dot(t_ref[...], updated, NT))
    weight_copy.wait()
    values = dot(updated, wv_s[...]).astype(BF16)
    partial_out(scores, values, mask, part_ref)
    out_copy.wait()


def update(returned, patches, w_out, turned, w_class):
    shapes = (
        jax.ShapeDtypeStruct((ROWS, D), BF16),
        jax.ShapeDtypeStruct((HEADS, 16, 128), F32),
    )
    scratch = (pltpu.VMEM((ROWS, D), BF16), SQUARE, pltpu.SemaphoreType.DMA((2,)))
    args = (returned, patches, turned, w_out)
    return call(update_kernel, "update", 4 * ROWS * D * D, shapes, args, (w_class,), scratch, 1)


def class_kv_kernel(upd_hbm, w_hbm, m_hbm, k_ref, v_ref, m_ref, upd_s, wk_s, wv_s, sems):
    copies = start_copies(
        [
            (upd_hbm, upd_s, sems.at[0]),
            (w_hbm.at[1, 1], wk_s, sems.at[1]),
            (w_hbm.at[1, 2], wv_s, sems.at[2]),
            (m_hbm.at[0], m_ref, sems.at[3]),
        ]
    )
    copies[0].wait()
    updated = upd_s[...]
    copies[1].wait()
    k_ref[...] = dot(updated, wk_s[...]).astype(BF16)
    copies[2].wait()
    v_ref[...] = dot(updated, wv_s[...]).astype(BF16)
    copies[3].wait()


def class_kv(updated, w_class, m):
    rows = jax.ShapeDtypeStruct((ROWS, D), BF16)
    shapes = (rows, rows, jax.ShapeDtypeStruct((D, D), BF16))
    scratch = (pltpu.VMEM((ROWS, D), BF16), SQUARE, SQUARE, pltpu.SemaphoreType.DMA((4,)))
    return call(class_kv_kernel, "class_kv", 2**31, shapes, (), (updated, w_class, m), scratch)


def middle_kernel(parts_ref, self_ref, base_ref, m_ref, k_ref, v_ref, attn_ref, q_ref, part_ref):
    mask = head_mask()
    attn = combine(parts_ref, self_ref)
    attn_ref[...] = attn.astype(F32)
    query = ((base_ref[...] + dot(attn, m_ref[...])) * 0.125).astype(BF16).astype(F32)
    q_ref[...] = query
    spread_query = jnp.where(mask, query, 0.0).astype(BF16)
    scores = dot(spread_query, k_ref[...], NT) * LOG2E
    partial_out(scores, v_ref[...], mask, part_ref)


def middle(parts, self_part, base, m, keys, values):
    shapes = (
        jax.ShapeDtypeStruct((1, D), F32),
        jax.ShapeDtypeStruct((1, D), F32),
        jax.ShapeDtypeStruct((HEADS, 16, 128), F32),
    )
    return call(middle_kernel, "middle", 2**28, shapes, (parts, self_part, base, m, keys, values))


def self_kernel(cls_ref, attn_ref, q_ref, w_hbm, self_ref, cls_out_ref, wo_ref, w_s, sems):
    copies = start_copies(
        [
            (w_hbm.at[0, 3], w_s.at[0], sems.at[0]),
            (w_hbm.at[1, 1], w_s.at[1], sems.at[1]),
            (w_hbm.at[1, 2], w_s.at[2], sems.at[2]),
            (w_hbm.at[1, 3], wo_ref, sems.at[3]),
        ]
    )
    copies[0].wait()
    cls_token = cls_ref[...] + dot(attn_ref[...].astype(BF16), w_s[0])
    cls_out_ref[...] = cls_token
    copies[1].wait()
    copies[2].wait()
    value, score = self_terms(q_ref[...], cls_token.astype(BF16), w_s[1], w_s[2], head_mask())
    self_ref[0:8, :] = value
    self_ref[8:16, :] = score
    copies[3].wait()


def self_part(cls_in, attn, query, w_class):
    shapes = (
        jax.ShapeDtypeStruct((16, 128), F32),
        jax.ShapeDtypeStruct((1, D), F32),
        jax.ShapeDtypeStruct((D, D), BF16),
    )
    scratch = (pltpu.VMEM((3, D, D), BF16), pltpu.SemaphoreType.DMA((4,)))
    return call(self_kernel, "self_part", 2**30, shapes, (cls_in, attn, query), (w_class,), scratch)


def last_kernel(parts_ref, self_ref, cls_ref, wo_ref, out_ref):
    attn = combine(parts_ref, self_ref)
    out_ref[...] = cls_ref[...] + dot(attn, wo_ref[...])


def last(parts, self_terms_1, cls_token, w_o):
    shape = jax.ShapeDtypeStruct((1, D), F32)
    return call(last_kernel, "last", 2**27, shape, (parts, self_terms_1, cls_token, w_o))


def exchange(blocks):
    return lax.all_to_all(blocks, "patch", 0, 0)


def per_device(patches, cls_in, w_attn, w_out, w_class):
    qkv, turned, self_0, base, m = project(patches, w_attn, cls_in, w_class)
    qkv = exchange(qkv)
    returned = exchange(attend(qkv))
    turned, self_0, base, m = ahead(cls_in, turned, self_0, base, m, w_class)
    updated, part_0 = update(returned, patches, w_out, turned, w_class)
    parts_0 = exchange(part_0)
    keys, values, m = class_kv(updated, w_class, m)
    attn_0, query_1, part_1 = middle(parts_0, self_0, base, m, keys, values)
    parts_1 = exchange(part_1)
    self_1, cls_1, w_o_1 = self_part(cls_in, attn_0, query_1, w_class)
    return (updated, last(parts_1, self_1, cls_1, w_o_1))


def solution(mesh):
    placed = (P(("dp", "patch"), None), P("dp", None), P(), P(), P())
    return jax.shard_map(
        per_device,
        mesh=mesh,
        in_specs=placed,
        out_specs=(P(("dp", "patch"), None), P("dp", None)),
        check_vma=False,
    )
```

```python
import functools

import jax
import jax.numpy as jnp
from jax import lax
from jax.experimental import pallas as pl
from jax.experimental.pallas import tpu as pltpu
from jax.sharding import PartitionSpec as P

HEADS = 16
HEAD_DIM = 64
D = 1024
ROWS = 256
PATCHES = 4096
LOG2E = 1.4426950408889634
BF16 = jnp.bfloat16
F32 = jnp.float32
NN = (((1,), (0,)), ((), ()))
NT = (((1,), (1,)), ((), ()))
TN = (((0,), (0,)), ((), ()))
VMEM_LIMIT = 14 * 2**20
SMALL_LIMIT = 8 * 2**20
LARGE_LIMIT = 46 * 2**20
PROJECT_LIMIT = 50 * 2**20


def dot(a, b, dims=NN):
    return lax.dot_general(a, b, dims, preferred_element_type=F32)


RESIDENT = pl.BlockSpec(memory_space=pltpu.VMEM)
ANYWHERE = pl.BlockSpec(memory_space=pl.ANY)


def call(kernel, name, flops, out_shape, resident, remote=(), scratch=(), hbm_out=0):
    single = not isinstance(out_shape, tuple)
    count = 1 if single else len(out_shape)
    out_specs = (ANYWHERE,) * hbm_out + (RESIDENT,) * (count - hbm_out)
    return pl.pallas_call(
        kernel,
        out_shape=out_shape,
        in_specs=[RESIDENT] * len(resident) + [ANYWHERE] * len(remote),
        out_specs=out_specs[0] if single else out_specs,
        scratch_shapes=scratch,
        compiler_params=pltpu.CompilerParams(
            vmem_limit_bytes=LARGE_LIMIT if remote else SMALL_LIMIT
        ),
        cost_estimate=pl.CostEstimate(flops=flops, bytes_accessed=2**20, transcendentals=0),
        name=name,
    )(*resident, *remote)


SQUARE = pltpu.VMEM((D, D), BF16)


def head_mask():
    row = lax.broadcasted_iota(jnp.int32, (HEADS, D), 0)
    lane = lax.broadcasted_iota(jnp.int32, (HEADS, D), 1)
    return lane // HEAD_DIM == row


def split_rows(value):
    high = value.astype(BF16)
    low = (value - high.astype(F32)).astype(BF16)
    return jnp.concatenate([high, low], axis=0)


def fold_halves(value):
    return value[:HEADS] + value[HEADS:]


def spread(column, mask):
    return jnp.sum(jnp.where(mask, column, 0.0), axis=0, keepdims=True)


def to_tile(row):
    return jnp.concatenate([row[:, 128 * j : 128 * (j + 1)] for j in range(8)], axis=0)


def to_row(tile):
    return jnp.concatenate([tile[j : j + 1, :] for j in range(8)], axis=1)


def second_core():
    return lax.rem(lax.axis_index("dp"), 2) == 1


def project_kernel(
    x_ref, w_hbm, cls_hbm, class_hbm, out_ref, t_ref, self_ref, base_ref, m_hbm, w_s, m_s, cls_s, sems, sem
):
    copies = start_copies([(w_hbm.at[k], w_s.at[k], sems.at[k]) for k in range(2)])
    x = x_ref[...]
    for kind in range(3):
        copies[kind].wait()
        if kind == 0:
            copies += start_copies([(w_hbm.at[2], w_s.at[2], sems.at[2])])
        y = dot(x, w_s[kind])
        if kind == 0:
            y = y * (0.125 * LOG2E)
        yt = y.astype(BF16).T
        for h in range(HEADS):
            out_ref[h, kind * HEAD_DIM : (kind + 1) * HEAD_DIM, :] = yt[
                h * HEAD_DIM : (h + 1) * HEAD_DIM
            ]

    @pl.when(second_core())
    def _():
        (copy,) = start_copies([(cls_hbm, cls_s, sem)])
        copy.wait()
        class_ahead(cls_s[...], class_hbm, t_ref, self_ref, base_ref, m_hbm, w_s, m_s, sems, sem)


AHEAD_SHAPES = (
    jax.ShapeDtypeStruct((2 * HEADS, D), BF16),
    jax.ShapeDtypeStruct((16, 128), F32),
    jax.ShapeDtypeStruct((1, D), F32),
    jax.ShapeDtypeStruct((3, D, D), BF16),
)


def project(patches, w_attn, cls_in, w_class):
    return pl.pallas_call(
        project_kernel,
        out_shape=(jax.ShapeDtypeStruct((HEADS, 3 * HEAD_DIM, ROWS), BF16), *AHEAD_SHAPES),
        in_specs=[RESIDENT, ANYWHERE, ANYWHERE, ANYWHERE],
        out_specs=(RESIDENT, RESIDENT, RESIDENT, RESIDENT, ANYWHERE),
        scratch_shapes=[
            pltpu.VMEM((5, D, D), BF16),
            pltpu.VMEM((D, D), BF16),
            pltpu.VMEM((1, D), F32),
            pltpu.SemaphoreType.DMA((5,)),
            pltpu.SemaphoreType.DMA(()),
        ],
        compiler_params=pltpu.CompilerParams(vmem_limit_bytes=PROJECT_LIMIT),
        cost_estimate=pl.CostEstimate(
            flops=2 * ROWS * D * 3 * D, bytes_accessed=8 * 2**20, transcendentals=0
        ),
        name="project",
    )(patches, w_attn, cls_in, w_class)


CHUNK = 256
SPANS = [slice(c * CHUNK, (c + 1) * CHUNK) for c in range(PATCHES // CHUNK)]


def attend_kernel(qkv_ref, out_hbm, k_s, v_s, s_s, out_s, sems):
    for j, span in enumerate(SPANS):
        k_s[span, :] = qkv_ref[j, 64:128, :].T
        v_s[0:64, span] = qkv_ref[j, 128:192, :]
    v_s[64:80, :] = jnp.ones((16, PATCHES), BF16)

    def scores_of(q_t, span, now):
        scores = dot(k_s[span, :], q_t)
        s_s[now, span, :] = scores
        return jnp.max(scores, axis=0, keepdims=True)

    def weigh(span, before, top):
        probs = jnp.exp2(s_s[before, span, :] - top).astype(BF16)
        return dot(v_s[:, span], probs)

    def leave(block):
        return pltpu.make_async_copy(out_s.at[block], out_hbm.at[block], sems.at[block])

    def finish(block, total):
        out_s[block] = (total[0:64] / total[64:65]).astype(BF16)
        leave(block).start()

    def both(block, now, top):
        q_t = qkv_ref[block, 0:64, :]
        total = jnp.zeros((80, ROWS), F32)
        tops = []
        for span in SPANS:
            tops.append(scores_of(q_t, span, now))
            total = total + weigh(span, 1 - now, top)
        finish(block - 1, total)
        return functools.reduce(jnp.maximum, tops)

    def pair(t, top):
        top = both(2 * t + 1, 1, top)
        return both(2 * t + 2, 0, top)

    q_t = qkv_ref[0, 0:64, :]
    top = functools.reduce(jnp.maximum, [scores_of(q_t, span, 0) for span in SPANS])
    top = lax.fori_loop(0, 7, pair, top)
    top = both(15, 1, top)
    total = jnp.zeros((80, ROWS), F32)
    for span in SPANS:
        total = total + weigh(span, 1, top)
    finish(15, total)
    for block in range(HEADS):
        leave(block).wait()


def attend(qkv):
    return pl.pallas_call(
        attend_kernel,
        out_shape=jax.ShapeDtypeStruct((HEADS, HEAD_DIM, ROWS), BF16),
        in_specs=[RESIDENT],
        out_specs=ANYWHERE,
        scratch_shapes=[
            pltpu.VMEM((PATCHES, HEAD_DIM), BF16),
            pltpu.VMEM((80, PATCHES), BF16),
            pltpu.VMEM((2, PATCHES, ROWS), F32),
            pltpu.VMEM((HEADS, HEAD_DIM, ROWS), BF16),
            pltpu.SemaphoreType.DMA((HEADS,)),
        ],
        compiler_params=pltpu.CompilerParams(vmem_limit_bytes=VMEM_LIMIT),
        cost_estimate=pl.CostEstimate(
            flops=16 * PATCHES * PATCHES * HEAD_DIM, bytes_accessed=2**21, transcendentals=PATCHES**2
        ),
        name="attend",
    )(qkv)


def self_terms(query, cls_bf16, wk, wv, mask):
    self_key = dot(cls_bf16, wk)
    self_value = dot(cls_bf16, wv)
    product = jnp.where(mask, query * self_key, 0.0)
    score = jnp.sum(product, axis=1, keepdims=True) * LOG2E
    return to_tile(self_value), to_tile(spread(score, mask))


def class_query(cls_bf16, wq):
    return (dot(cls_bf16, wq) * 0.125).astype(BF16).astype(F32)


def start_copies(copies):
    copies = [pltpu.make_async_copy(*copy) for copy in copies]
    for copy in copies:
        copy.start()
    return copies


def class_ahead(cls_token, w_hbm, t_ref, self_ref, base_ref, m_hbm, w_s, m_s, sems, sem):
    sources = ((0, 0), (0, 1), (0, 2), (0, 3), (1, 0))
    copies = start_copies([(w_hbm.at[c, k], w_s.at[n], sems.at[n]) for n, (c, k) in enumerate(sources)])
    mask = head_mask()
    cls_bf16 = cls_token.astype(BF16)
    copies[0].wait()
    query = class_query(cls_bf16, w_s[0])
    spread_query = jnp.where(mask, query, 0.0).astype(BF16)
    copies[1].wait()
    turned = dot(spread_query, w_s[1], NT) * LOG2E
    t_ref[...] = split_rows(turned)
    copies[2].wait()
    value, score = self_terms(query, cls_bf16, w_s[1], w_s[2], mask)
    self_ref[0:8, :] = value
    self_ref[8:16, :] = score
    copies[3].wait()
    copies[4].wait()
    low = (cls_token - cls_bf16.astype(F32)).astype(BF16)
    base_ref[...] = dot(cls_bf16, w_s[4]) + dot(low, w_s[4])
    for c in range(4):
        rows = slice(c * 256, (c + 1) * 256)
        m_s[rows, :] = dot(w_s[3, rows, :], w_s[4]).astype(BF16)
    (copy,) = start_copies([(m_s, m_hbm.at[0], sem)])
    copy.wait()


def ahead_kernel(
    cls_ref, t_in, self_in, base_in, w_hbm, m_in, t_ref, self_ref, base_ref, m_hbm, w_s, m_s, sems, sem
):
    del m_in
    second = second_core()

    @pl.when(second)
    def _():
        t_ref[...] = t_in[...]
        self_ref[...] = self_in[...]
        base_ref[...] = base_in[...]

    @pl.when(jnp.logical_not(second))
    def _():
        class_ahead(cls_ref[...], w_hbm, t_ref, self_ref, base_ref, m_hbm, w_s, m_s, sems, sem)


def ahead(cls_in, turned, self_0, base, m, w_class):
    return pl.pallas_call(
        ahead_kernel,
        out_shape=AHEAD_SHAPES,
        in_specs=[RESIDENT] * 4 + [ANYWHERE] * 2,
        out_specs=(RESIDENT, RESIDENT, RESIDENT, ANYWHERE),
        scratch_shapes=[
            pltpu.VMEM((5, D, D), BF16),
            SQUARE,
            pltpu.SemaphoreType.DMA((5,)),
            pltpu.SemaphoreType.DMA(()),
        ],
        input_output_aliases={5: 3},
        compiler_params=pltpu.CompilerParams(vmem_limit_bytes=49 * 2**20),
        cost_estimate=pl.CostEstimate(flops=2**32, bytes_accessed=2**20, transcendentals=0),
        name="ahead",
    )(cls_in, turned, self_0, base, w_class, m)


def partial_out(scores, values, mask, out_ref):
    top = jnp.max(scores, axis=1, keepdims=True)
    terms = jnp.exp2(scores - top)
    total = jnp.sum(terms, axis=1, keepdims=True)
    weighted = fold_halves(dot(split_rows(terms), values)) / total
    row = jnp.sum(jnp.where(mask, weighted, 0.0), axis=0, keepdims=True)
    tile = jnp.concatenate([to_tile(row), to_tile(spread(top + jnp.log2(total), mask))], axis=0)
    for d in range(HEADS):
        out_ref[d] = tile


def combine(parts_ref, self_ref):
    top = self_ref[8:16, :]
    for d in range(HEADS):
        top = jnp.maximum(top, parts_ref[d, 8:16, :])
    weight = jnp.exp2(self_ref[8:16, :] - top)
    total = weight
    value = weight * self_ref[0:8, :]
    for d in range(HEADS):
        weight = jnp.exp2(parts_ref[d, 8:16, :] - top)
        total = total + weight
        value = value + weight * parts_ref[d, 0:8, :]
    return to_row(value / total).astype(BF16)


def update_kernel(ret_ref, x_ref, t_ref, wo_ref, w_hbm, upd_hbm, part_ref, upd_s, wv_s, sems):
    (weight_copy,) = start_copies([(w_hbm.at[0, 2], wv_s, sems.at[0])])
    mask = head_mask()
    attended = ret_ref[...].reshape(D, ROWS)
    updated = (x_ref[...].astype(F32) + dot(attended, wo_ref[...], TN)).astype(BF16)
    upd_s[...] = updated
    (out_copy,) = start_copies([(upd_s, upd_hbm, sems.at[1])])
    scores = fold_halves(dot(t_ref[...], updated, NT))
    weight_copy.wait()
    values = dot(updated, wv_s[...]).astype(BF16)
    partial_out(scores, values, mask, part_ref)
    out_copy.wait()


def update(returned, patches, w_out, turned, w_class):
    shapes = (
        jax.ShapeDtypeStruct((ROWS, D), BF16),
        jax.ShapeDtypeStruct((HEADS, 16, 128), F32),
    )
    scratch = (pltpu.VMEM((ROWS, D), BF16), SQUARE, pltpu.SemaphoreType.DMA((2,)))
    args = (returned, patches, turned, w_out)
    return call(update_kernel, "update", 4 * ROWS * D * D, shapes, args, (w_class,), scratch, 1)


def class_kv_kernel(upd_hbm, w_hbm, m_hbm, k_ref, v_ref, m_ref, upd_s, wk_s, wv_s, sems):
    copies = start_copies(
        [
            (upd_hbm, upd_s, sems.at[0]),
            (w_hbm.at[1, 1], wk_s, sems.at[1]),
            (w_hbm.at[1, 2], wv_s, sems.at[2]),
            (m_hbm.at[0], m_ref, sems.at[3]),
        ]
    )
    copies[0].wait()
    updated = upd_s[...]
    copies[1].wait()
    k_ref[...] = dot(updated, wk_s[...]).astype(BF16)
    copies[2].wait()
    v_ref[...] = dot(updated, wv_s[...]).astype(BF16)
    copies[3].wait()


def class_kv(updated, w_class, m):
    rows = jax.ShapeDtypeStruct((ROWS, D), BF16)
    shapes = (rows, rows, jax.ShapeDtypeStruct((D, D), BF16))
    scratch = (pltpu.VMEM((ROWS, D), BF16), SQUARE, SQUARE, pltpu.SemaphoreType.DMA((4,)))
    return call(class_kv_kernel, "class_kv", 2**31, shapes, (), (updated, w_class, m), scratch)


def middle_kernel(parts_ref, self_ref, base_ref, m_ref, k_ref, v_ref, attn_ref, q_ref, part_ref):
    mask = head_mask()
    attn = combine(parts_ref, self_ref)
    attn_ref[...] = attn.astype(F32)
    query = ((base_ref[...] + dot(attn, m_ref[...])) * 0.125).astype(BF16).astype(F32)
    q_ref[...] = query
    spread_query = jnp.where(mask, query, 0.0).astype(BF16)
    scores = dot(spread_query, k_ref[...], NT) * LOG2E
    partial_out(scores, v_ref[...], mask, part_ref)


def middle(parts, self_part, base, m, keys, values):
    shapes = (
        jax.ShapeDtypeStruct((1, D), F32),
        jax.ShapeDtypeStruct((1, D), F32),
        jax.ShapeDtypeStruct((HEADS, 16, 128), F32),
    )
    return call(middle_kernel, "middle", 2**28, shapes, (parts, self_part, base, m, keys, values))


def self_kernel(cls_ref, attn_ref, q_ref, w_hbm, self_ref, cls_out_ref, wo_ref, w_s, sems):
    copies = start_copies(
        [
            (w_hbm.at[0, 3], w_s.at[0], sems.at[0]),
            (w_hbm.at[1, 1], w_s.at[1], sems.at[1]),
            (w_hbm.at[1, 2], w_s.at[2], sems.at[2]),
            (w_hbm.at[1, 3], wo_ref, sems.at[3]),
        ]
    )
    copies[0].wait()
    cls_token = cls_ref[...] + dot(attn_ref[...].astype(BF16), w_s[0])
    cls_out_ref[...] = cls_token
    copies[1].wait()
    copies[2].wait()
    value, score = self_terms(q_ref[...], cls_token.astype(BF16), w_s[1], w_s[2], head_mask())
    self_ref[0:8, :] = value
    self_ref[8:16, :] = score
    copies[3].wait()


def self_part(cls_in, attn, query, w_class):
    shapes = (
        jax.ShapeDtypeStruct((16, 128), F32),
        jax.ShapeDtypeStruct((1, D), F32),
        jax.ShapeDtypeStruct((D, D), BF16),
    )
    scratch = (pltpu.VMEM((3, D, D), BF16), pltpu.SemaphoreType.DMA((4,)))
    return call(self_kernel, "self_part", 2**30, shapes, (cls_in, attn, query), (w_class,), scratch)


def last_kernel(parts_ref, self_ref, cls_ref, wo_ref, out_ref):
    attn = combine(parts_ref, self_ref)
    out_ref[...] = cls_ref[...] + dot(attn, wo_ref[...])


def last(parts, self_terms_1, cls_token, w_o):
    shape = jax.ShapeDtypeStruct((1, D), F32)
    return call(last_kernel, "last", 2**27, shape, (parts, self_terms_1, cls_token, w_o))


def exchange(blocks):
    return lax.all_to_all(blocks, "patch", 0, 0)


def per_device(patches, cls_in, w_attn, w_out, w_class):
    qkv, turned, self_0, base, m = project(patches, w_attn, cls_in, w_class)
    qkv = exchange(qkv)
    returned = exchange(attend(qkv))
    turned, self_0, base, m = ahead(cls_in, turned, self_0, base, m, w_class)
    updated, part_0 = update(returned, patches, w_out, turned, w_class)
    parts_0 = exchange(part_0)
    keys, values, m = class_kv(updated, w_class, m)
    attn_0, query_1, part_1 = middle(parts_0, self_0, base, m, keys, values)
    parts_1 = exchange(part_1)
    self_1, cls_1, w_o_1 = self_part(cls_in, attn_0, query_1, w_class)
    return (updated, last(parts_1, self_1, cls_1, w_o_1))


def solution(mesh):
    placed = (P(("dp", "patch"), None), P("dp", None), P(), P(), P())
    return jax.shard_map(
        per_device,
        mesh=mesh,
        in_specs=placed,
        out_specs=(P(("dp", "patch"), None), P("dp", None)),
        check_vma=False,
    )
```
